256 devices in a mesh: chan: 128 (over x_hi, y, z, core), tile: 2 (over x_lo).
Axes of the slice: x: 4 (x_hi: 2, x_lo: 2; x = x_hi * 2 + x_lo), y: 4, z: 8, core: 2. Of those that a mesh axis runs over, the one named last changes fastest.
Arguments:
- raw_strain: bfloat16 [4096, 131072], P(('chan', 'tile')), may hold values from -6 to 6
- fir_taps: bfloat16 [128], replicated, may hold values from -0.5 to 0.5
- fan_band: int32 [4096, 256], P(None, 'tile'), may hold values from 0 to 7
- band_gain: float32 [8], replicated, may hold values from 0 to 1
Outputs:
- filtered: float32 [4096, 32768], P(('chan', 'tile'))
The draws below stay inside these ranges and needn't reach their ends.
All inputs are finite; a program needn't handle non-finite values.
Results may differ from the reference program's by a relative error of at most 0.0003.
Values sent between devices are 32-bit elements; how exact they have to be, the bound alone decides.
No kernel may reach another device: no remote copies, remote signals or barrier semaphores. Data moves between devices by JAX's collectives and lax.ppermute only.
A program may use at most 64 MiB of HBM per device.

```python
import jax
import jax.numpy as jnp
from jax import lax

K = 4096
ROOT = 64
WIN = 512
TAPS = 128
DEC = 4
BANDS = 8
HOP = 256
BINS = 256
WINDOWS = 128
TD = 32768
TR = 131072


def with_ends(entries, rng, least, largest):
    longest = entries.shape.index(max(entries.shape))
    spots = []
    for shift in (0, 1):
        where = [jax.random.randint(jax.random.fold_in(rng, axis), (), 0, length) for axis, length in enumerate(entries.shape)]
        where[longest] = (where[longest] + shift) % entries.shape[longest]
        spots.append(tuple(where))
    return entries.at[spots[0]].set(least).at[spots[1]].set(largest)


def level_of(stream_key, extent, pieces, smallest, top_value):
    def one(dim, shards_of):
        heights = jax.random.uniform(jax.random.fold_in(jax.random.fold_in(stream_key, 6), dim), (shards_of,), jnp.float32, smallest / len(pieces), top_value / len(pieces))
        return jnp.repeat(jnp.exp(heights), extent[dim] // shards_of).reshape((-1,) + (1,) * (len(extent) - dim - 1))

    factor_of = one(*pieces[0])
    for cut in pieces[1:]:
        factor_of = factor_of * one(*cut)
    return factor_of


def gaussian(stream_key, shape, width, bound, split=(), kind=jnp.bfloat16):
    factor_of = level_of(stream_key, shape, split, -0.22, 0.18) if split else 1.0
    values = jax.random.normal(stream_key, shape, jnp.float32) * width * factor_of
    return jnp.minimum(jnp.maximum(values, -bound), bound).astype(kind)


def setup_inputs(seed: int = 0) -> dict:
    keys = jax.random.split(jax.random.key(seed), 5)
    raw_strain = gaussian(keys[0], (K, TR), 1.0, 6.0, ((0, 256),))
    fir_taps = gaussian(keys[1], (TAPS,), TAPS ** -0.5, 0.5)
    fan_band = with_ends(jax.random.randint(keys[2], (K, BINS), 0, BANDS), jax.random.fold_in(keys[2], 1), 0, BANDS - 1).astype(jnp.int32)
    band_gain = jnp.clip(jax.random.uniform(keys[3], (BANDS,), jnp.float32, 0.0, 1.0), 0.0, 1.0)
    return dict(raw_strain=raw_strain, fir_taps=fir_taps, fan_band=fan_band, band_gain=band_gain)


def decimate_all(raw_strain, fir_taps):
    kernel = fir_taps.astype(jnp.float32)[::-1].reshape(1, 1, TAPS)

    def fir_group(channel_rows):
        signal = channel_rows.astype(jnp.float32)[:, None, :]
        result = lax.conv_general_dilated(signal, kernel, (DEC,), [(TAPS - 1, 0)], precision=lax.Precision.HIGHEST)
        return result[:, 0, :]

    grouped = raw_strain.reshape(ROOT, ROOT, DEC * TD)
    return lax.map(fir_group, grouped).reshape(K, TD)


def reference(raw_strain, fir_taps, fan_band, band_gain):
    decimated = decimate_all(raw_strain, fir_taps)
    rim_width = HOP // 2
    padded = jnp.pad(decimated, ((0, 0), (rim_width, rim_width)))
    sample = jnp.arange(WIN).astype(jnp.float32)
    sine_taper = jnp.sin(jnp.pi * (sample + 0.5) / WIN)
    bin_gains = band_gain[fan_band]
    column_mask = (jnp.arange(BINS) > 0).astype(jnp.float32)

    def add_window(window_index, accumulated):
        start_at = (window_index * HOP).astype(jnp.int32)
        segment = lax.dynamic_slice_in_dim(padded, start_at, WIN, 1) * sine_taper
        spectrum = jnp.fft.rfft(segment, axis=1)[:, :BINS]
        wave_domain = jnp.fft.fft(spectrum, axis=0) * bin_gains
        restored = jnp.fft.ifft(wave_domain, axis=0)
        restored = lax.complex(jnp.real(restored), jnp.imag(restored) * column_mask)
        restored = jnp.pad(restored, ((0, 0), (0, 1)))
        window_out = jnp.fft.irfft(restored, n=WIN, axis=1) * sine_taper
        current = lax.dynamic_slice_in_dim(accumulated, start_at, WIN, 1)
        return lax.dynamic_update_slice_in_dim(accumulated, current + window_out, start_at, 1)

    accumulated = lax.fori_loop(0, WINDOWS, add_window, jnp.zeros((K, TD + HOP), jnp.float32))
    return accumulated[:, rim_width:rim_width + TD]
```

```python
import math

import jax
import jax.numpy as jnp
import numpy as np
from jax import lax
from jax.experimental import pallas as pl
from jax.experimental.pallas import tpu as pltpu
from jax.sharding import PartitionSpec as P
import ml_dtypes

K = 4096
ROOT = 64
WIN = 512
TAPS = 128
DEC = 4
BANDS = 8
HOP = 256
BINS = 256
BLK = 128
SLOTS = 32
HALF = 16
AXES = ("chan", "tile")
F32 = jnp.float32
BF16 = jnp.bfloat16
BIG = 60 * 1024 * 1024


def two(table):
    table = np.asarray(table, np.float32)
    hi = table.astype(ml_dtypes.bfloat16)
    lo = (table - hi.astype(np.float32)).astype(ml_dtypes.bfloat16)
    return hi, lo


def left_operand(table):
    hi, lo = two(table)
    return np.concatenate([hi, hi, lo], axis=-1)


def own_first(table, axis):
    other = np.roll(table, -HALF, axis=axis)
    return np.stack([table, other], axis=0)


def spatial_tables():
    c1 = np.arange(ROOT)
    slot = np.arange(SLOTS)[:, None]
    angle = 2 * np.pi / ROOT * (slot * c1 % ROOT)
    re, im = np.cos(angle), np.sin(angle)
    im[0] = -((-1.0) ** c1)
    first = np.stack([re, -im], axis=0)
    first = own_first(first, 1).reshape(2, ROOT, ROOT)
    c0 = np.arange(ROOT)[None, :]
    k2 = np.arange(ROOT)[:, None]
    second = np.zeros((SLOTS, 2, ROOT, 2, ROOT))
    inverse = np.zeros((SLOTS, 2, ROOT, 2, ROOT))
    for s in range(SLOTS):
        phase = 2 * np.pi / K * ((s + ROOT * k2) * c0 % K)
        co, si = np.cos(phase), np.sin(phase)
        if s:
            second[s, 0, :, 0], second[s, 0, :, 1] = co, si
            second[s, 1, :, 0], second[s, 1, :, 1] = -si, co
            inverse[s, 0, :, 0], inverse[s, 0, :, 1] = co.T, -si.T
            inverse[s, 1, :, 0], inverse[s, 1, :, 1] = si.T, co.T
            continue
        n = ROOT // 2
        second[0, 0, :n, 0], second[0, 1, :n, 0] = co[:n], -si[:n]
        second[0, 1, 0, 0] = (-1.0) ** c0[0]
        inverse[0, 0, :, 0, :n], inverse[0, 0, :, 1, :n] = co[:n].T, -si[:n].T
        inverse[0, 0, :, 0, 0] = 0.5
        inverse[0, 0, :, 1, 0] = 0.5 * (-1.0) ** c0[0]
        phase = 2 * np.pi / K * ((n + ROOT * k2[:n]) * c0 % K)
        co, si = np.cos(phase), np.sin(phase)
        second[0, 0, n:, 1], second[0, 1, n:, 1] = co, -si
        inverse[0, 1, :, 0, n:], inverse[0, 1, :, 1, n:] = co.T, -si.T
    second = second.reshape(SLOTS, BLK, BLK)
    inverse = inverse.reshape(SLOTS, BLK, BLK) / K
    last = np.swapaxes(first, 1, 2)
    return (left_operand(first), left_operand(second), left_operand(inverse), left_operand(last))


def temporal_tables():
    s = np.arange(WIN)[:, None]
    f = np.arange(BINS)[None, :]
    angle = 2 * np.pi / WIN * (s * f % WIN)
    taper = np.sin(np.pi * (s + 0.5) / WIN)
    forward = np.concatenate([np.cos(angle), np.sin(angle)], axis=1) * taper
    weight = np.where(f == 0, 1.0, 2.0) / WIN
    backward = np.concatenate([np.cos(angle) * weight, np.sin(angle) * weight], axis=1) * taper
    return np.stack(two(forward)), np.stack(two(backward.T))


def chip_of(j):
    row, i = divmod(j, 4)
    z, q = divmod(row, 4)
    x = i if row % 2 == 0 else 3 - i
    y = q if z % 2 == 0 else 3 - q
    return x, y, z


def device_of(j, core):
    x, y, z = chip_of(j)
    return (((x // 2 * 4 + y) * 8 + z) * 2 + core) * 2 + x % 2


def permutes(windows):
    partner = [(device_of(j, c), device_of(j, 1 - c)) for j in range(windows) for c in (0, 1)]
    same, cross = [], []
    for j in range(windows - 1):
        same.append((device_of(j + 1, 0), device_of(j, 0)))
        same.append((device_of(j, 1), device_of(j + 1, 1)))
        cross.append((device_of(j + 1, 0), device_of(j, 1)))
        cross.append((device_of(j, 1), device_of(j + 1, 0)))
    return partner, same, cross


def flipped(pairs):
    return [(b, a) for a, b in pairs]


def split(value):
    hi = value.astype(BF16)
    return hi, (value - hi.astype(F32)).astype(BF16)


def stacked(value):
    hi, lo = split(value)
    return jnp.concatenate([hi, lo, hi], axis=0)


def dot(a, b):
    return jnp.dot(a, b, preferred_element_type=F32)


def plane_slot(b):
    j, core = divmod(b, 2)
    row, i = divmod(j, 4)
    x = i if row % 2 == 0 else 3 - i
    return x // 2, row, core, x % 2


def decimate_kernel(taps_ref, tail_ref, cur_ref, out_ref, band_ref):
    plane = pl.program_id(0)
    span = TAPS + DEC * BLK

    @pl.when(plane == 0)
    def _():
        i = lax.broadcasted_iota(jnp.int32, (TAPS, TAPS), 0)
        j = lax.broadcasted_iota(jnp.int32, (TAPS, TAPS), 1)
        mirror = (i + j == TAPS - 1).astype(BF16)
        mirrored = dot(taps_ref[...], mirror)
        rows = jnp.broadcast_to(mirrored[:1], (BLK, TAPS))
        wide = jnp.concatenate([rows, jnp.zeros((BLK, span - TAPS), F32)], axis=1)
        band_ref[...] = pltpu.roll(wide, 1, 1, stride=DEC, stride_axis=0).astype(BF16)

    tail = jnp.where(plane == 0, jnp.zeros_like(tail_ref[...]), tail_ref[...])
    blocks = cur_ref.shape[1] // (DEC * BLK)
    band = band_ref[...]
    group = 8
    for b0 in range(0, blocks, group):
        spans = []
        for b in range(b0, b0 + group):
            start = b * DEC * BLK
            if b == 0:
                spans.append(jnp.concatenate([tail, cur_ref[:, : DEC * BLK]], axis=1))
            else:
                spans.append(cur_ref[:, start - TAPS : start + DEC * BLK])
        result = lax.dot_general(
            jnp.concatenate(spans, axis=0), band, (((1,), (1,)), ((), ())), preferred_element_type=F32
        )
        for n in range(group):
            xh, row, core, xl = plane_slot(b0 + n)
            y = jnp.where(plane % 2 == 0, row, 3 - row)
            out_ref[xh, y, 0, core, xl] = result[n * 16 : (n + 1) * 16]


def decimate(raw, taps):
    channels, length = raw.shape
    planes = 8
    width = length // planes
    taps = jnp.broadcast_to(taps[None, :], (16, TAPS))
    return pl.pallas_call(
        decimate_kernel,
        grid=(planes,),
        in_specs=[
            pl.BlockSpec((16, TAPS), lambda g: (0, 0)),
            pl.BlockSpec((channels, TAPS), lambda g: (0, jnp.maximum(g * (width // TAPS) - 1, 0))),
            pl.BlockSpec((channels, width), lambda g: (0, g)),
        ],
        out_specs=pl.BlockSpec((2, 4, 1, 2, 2, channels, BLK), lambda g: (0, 0, g, 0, 0, 0, 0)),
        out_shape=jax.ShapeDtypeStruct((2, 4, planes, 2, 2, channels, BLK), F32),
        scratch_shapes=[pltpu.VMEM((BLK, TAPS + DEC * BLK), BF16)],
        compiler_params=pltpu.CompilerParams(vmem_limit_bytes=BIG),
        name="decimate",
    )(taps, raw, raw)


def unplane_kernel(in_ref, out_ref):
    plane = pl.program_id(0)
    for b in range(32):
        xh, row, core, xl = plane_slot(b)
        y = jnp.where(plane % 2 == 0, row, 3 - row)
        out_ref[:, b * BLK : (b + 1) * BLK] = in_ref[xh, y, 0, core, xl]


def unplane(blocks):
    planes = blocks.shape[2]
    channels = blocks.shape[5]
    return pl.pallas_call(
        unplane_kernel,
        grid=(planes,),
        in_specs=[pl.BlockSpec((2, 4, 1, 2, 2, channels, BLK), lambda g: (0, 0, g, 0, 0, 0, 0))],
        out_specs=pl.BlockSpec((channels, 32 * BLK), lambda g: (0, g)),
        out_shape=jax.ShapeDtypeStruct((channels, planes * 32 * BLK), F32),
        compiler_params=pltpu.CompilerParams(vmem_limit_bytes=BIG),
        name="unplane",
    )(blocks)


def forward_kernel(where_ref, x_ref, first_ref, second_ref, out_ref, mid_ref):
    core = where_ref[0]
    first = first_ref[core]
    for c0 in range(0, ROOT, 2):
        one = stacked(x_ref[pl.ds(c0, ROOT, stride=ROOT), :])
        two_ = stacked(x_ref[pl.ds(c0 + 1, ROOT, stride=ROOT), :])
        y = dot(first, jnp.concatenate([one, two_], axis=1))
        mid_ref[c0 * ROOT : (c0 + 1) * ROOT, :] = y[:, :BLK]
        mid_ref[(c0 + 1) * ROOT : (c0 + 2) * ROOT, :] = y[:, BLK:]
    for s in range(SLOTS):
        re = mid_ref[pl.ds(s, ROOT, stride=ROOT), :]
        im = mid_ref[pl.ds(SLOTS + s, ROOT, stride=ROOT), :]
        table = second_ref[lax.rem(s + HALF * core, SLOTS)]
        out_ref[s] = dot(table, stacked(jnp.concatenate([re, im], axis=0)))


def forward_space(where, x, first, second):
    return pl.pallas_call(
        forward_kernel,
        in_specs=[pl.BlockSpec(memory_space=pltpu.SMEM)] + [pl.BlockSpec(memory_space=pltpu.VMEM)] * 3,
        out_specs=pl.BlockSpec(memory_space=pltpu.VMEM),
        out_shape=jax.ShapeDtypeStruct((SLOTS, BLK, BLK), F32),
        scratch_shapes=[pltpu.VMEM((K, BLK), F32)],
        compiler_params=pltpu.CompilerParams(vmem_limit_bytes=BIG),
        name="forward_space",
    )(where, x, first, second)


def inverse_kernel(where_ref, own_ref, halo_ref, part_ref, cross_ref, inv_ref, last_ref, out_ref, mid_ref):
    core = where_ref[0]
    for s in range(SLOTS):
        if s < HALF:
            z = own_ref[s] + halo_ref[s]
        else:
            z = part_ref[s - HALF] + cross_ref[s - HALF]
        table = inv_ref[lax.rem(s + HALF * core, SLOTS)]
        u = dot(table, stacked(z))
        mid_ref[pl.ds(s, ROOT, stride=ROOT), :] = u[:ROOT]
        mid_ref[pl.ds(SLOTS + s, ROOT, stride=ROOT), :] = u[ROOT:]
    last = last_ref[core]
    for c0 in range(0, ROOT, 2):
        one = stacked(mid_ref[c0 * ROOT : (c0 + 1) * ROOT, :])
        two_ = stacked(mid_ref[(c0 + 1) * ROOT : (c0 + 2) * ROOT, :])
        y = dot(last, jnp.concatenate([one, two_], axis=1))
        out_ref[pl.ds(c0, ROOT, stride=ROOT), :] = y[:, :BLK]
        out_ref[pl.ds(c0 + 1, ROOT, stride=ROOT), :] = y[:, BLK:]


def inverse_space(where, own, halo, part, cross, inv, last):
    return pl.pallas_call(
        inverse_kernel,
        in_specs=[pl.BlockSpec(memory_space=pltpu.SMEM)] + [pl.BlockSpec(memory_space=pltpu.VMEM)] * 6,
        out_specs=pl.BlockSpec(memory_space=pltpu.VMEM),
        out_shape=jax.ShapeDtypeStruct((K, BLK), F32),
        scratch_shapes=[pltpu.VMEM((K, BLK), F32)],
        compiler_params=pltpu.CompilerParams(vmem_limit_bytes=BIG),
        name="inverse_space",
    )(where, own, halo, part, cross, inv, last)


def gains_kernel(where_ref, gain_ref, band_ref, out_ref):
    core = where_ref[0]
    n = ROOT // 2
    i = lax.broadcasted_iota(jnp.int32, (ROOT, ROOT), 0)
    j = lax.broadcasted_iota(jnp.int32, (ROOT, ROOT), 1)
    mirror = (i + j == ROOT - 1).astype(BF16)
    source = jnp.where(i == 0, 0, jnp.where(i < n, n - i, n + ROOT - 1 - i))
    mirror0 = (j == source).astype(BF16)

    def rows(k1, k2, count):
        return band_ref[pl.ds(k1 + ROOT * k2, count, stride=ROOT), :]

    def exact(perm, bands):
        return dot(perm, bands.astype(F32).astype(BF16))

    def pick(bands):
        total = jnp.zeros(bands.shape, F32)
        for b in range(BANDS):
            total = jnp.where(bands == b, gain_ref[b], total)
        return total

    def put(s, plus, minus):
        gp, gm = pick(plus.astype(F32)), pick(minus)
        out_ref[0, s] = gp + gm
        out_ref[1, s] = gp - gm

    for s in range(HALF):
        if s:
            k1 = s + HALF * core
            put(s, rows(k1, 0, ROOT), exact(mirror, rows(ROOT - k1, 0, ROOT)))
            continue

        @pl.when(core == 0)
        def _():
            plus = jnp.concatenate([rows(0, 0, n), rows(n, 0, n)], axis=0)
            minus = jnp.concatenate([rows(0, n, n), rows(n, n, n)], axis=0)
            put(0, plus, exact(mirror0, minus))

        @pl.when(core != 0)
        def _():
            put(0, rows(HALF, 0, ROOT), exact(mirror, rows(ROOT - HALF, 0, ROOT)))


def gains(where, band_gain, fan_band):
    return pl.pallas_call(
        gains_kernel,
        in_specs=[pl.BlockSpec(memory_space=pltpu.SMEM)] * 2 + [pl.BlockSpec(memory_space=pltpu.VMEM)],
        out_specs=pl.BlockSpec(memory_space=pltpu.VMEM),
        out_shape=jax.ShapeDtypeStruct((2, HALF, ROOT, BLK), F32),
        compiler_params=pltpu.CompilerParams(vmem_limit_bytes=BIG),
        name="gains",
    )(where, band_gain, fan_band)


def time_kernel(where_ref, own_ref, part_ref, same_ref, cross_ref, mine_ref, theirs_ref, fwd_ref, bwd_ref, out_ref):
    core, xl = where_ref[0], where_ref[1]
    step = pl.program_id(0)
    slots = own_ref.shape[0]
    rows = slots * BLK
    even = core == 0

    def flat(ref):
        return ref[...].reshape(rows, BLK)

    own, part, same, cross = flat(own_ref), flat(part_ref), flat(same_ref), flat(cross_ref)
    x = jnp.concatenate(
        [
            jnp.where(even, cross, same),
            jnp.where(even, own, part),
            jnp.where(even, part, own),
            jnp.where(even, same, cross),
        ],
        axis=1,
    )
    hi, lo = split(x)
    fwd_hi = fwd_ref[0]
    v = dot(hi, fwd_hi) + dot(lo, fwd_hi) + dot(hi, fwd_ref[1])
    pieces = []
    for s in range(slots):
        p = v[s * BLK : s * BLK + ROOT]
        q = v[s * BLK + ROOT : (s + 1) * BLK]
        a, d = p[:, :BINS], p[:, BINS:]
        c, b = q[:, :BINS], q[:, BINS:]

        def wide(kind):
            mine, theirs = mine_ref[kind, s], theirs_ref[kind, s]
            low = jnp.where(xl == 0, mine, theirs)
            high = jnp.where(xl == 0, theirs, mine)
            return jnp.concatenate([low, high], axis=1)

        gs, gd = wide(0), wide(1)
        gr = gi = gs
        if s == 0:
            row = lax.broadcasted_iota(jnp.int32, (ROOT, BINS), 0)
            pair = (row == 0) & (step == 0) & even
            gr = jnp.where(pair, gs + gd, gs)
            gi = jnp.where(pair, gs - gd, gs)
            gd = jnp.where(pair, 0.0, gd)
        pieces.append(jnp.concatenate([gr * a + gd * b, gr * d - gd * c], axis=1))
        pieces.append(jnp.concatenate([gi * c - gd * d, gd * a + gi * b], axis=1))
    hi, lo = split(jnp.concatenate(pieces, axis=0))
    bwd_hi = bwd_ref[0]
    z = dot(hi, bwd_hi) + dot(lo, bwd_hi) + dot(hi, bwd_ref[1])
    places = [
        jnp.where(even, 3, 2),
        jnp.where(even, 0, 1),
        jnp.where(even, 1, 0),
        jnp.where(even, 2, 3),
    ]
    for n in range(4):
        out_ref[places[n]] = z[:, n * BLK : (n + 1) * BLK].reshape(slots, BLK, BLK)


def time_filter(where, own, part, same, cross, mine, theirs, fwd, bwd):
    total = own.shape[0]
    slots = 4
    data = pl.BlockSpec((slots, BLK, BLK), lambda g: (g, 0, 0))
    gain = pl.BlockSpec((2, slots, ROOT, BLK), lambda g: (0, g, 0, 0))
    table = pl.BlockSpec((2, WIN, WIN), lambda g: (0, 0, 0))
    return pl.pallas_call(
        time_kernel,
        grid=(total // slots,),
        in_specs=[pl.BlockSpec(memory_space=pltpu.SMEM)] + [data] * 4 + [gain] * 2 + [table] * 2,
        out_specs=pl.BlockSpec((4, slots, BLK, BLK), lambda g: (0, g, 0, 0)),
        out_shape=jax.ShapeDtypeStruct((4, total, BLK, BLK), F32),
        compiler_params=pltpu.CompilerParams(vmem_limit_bytes=BIG),
        name="time_filter",
    )(where, own, part, same, cross, mine, theirs, fwd, bwd)


def body(raw_strain, fir_taps, fan_band, band_gain):
    where = jnp.stack([lax.axis_index("chan") % 2, lax.axis_index("tile")]).astype(jnp.int32)
    first, second, inverse, last = (jnp.asarray(t) for t in spatial_tables())
    fwd, bwd = (jnp.asarray(t) for t in temporal_tables())
    partner, same, cross = permutes(raw_strain.shape[1] // DEC // HOP)

    mine = gains(where, band_gain, fan_band)
    theirs = lax.ppermute(mine, "tile", [(0, 1), (1, 0)])

    blocks = decimate(raw_strain, fir_taps)
    shape = blocks.shape
    blocks = blocks.reshape((256,) + shape[5:])
    blocks = lax.all_to_all(blocks, AXES, 0, 0, tiled=True)
    waves = forward_space(where, blocks.reshape(K, BLK), first, second)
    own, other = waves[:HALF], waves[HALF:]
    from_partner = lax.ppermute(other, AXES, partner)
    from_same = lax.ppermute(own, AXES, same)
    from_cross = lax.ppermute(other, AXES, cross)
    z = time_filter(where, own, from_partner, from_same, from_cross, mine, theirs, fwd, bwd)
    back_partner = lax.ppermute(z[1], AXES, partner)
    back_same = lax.ppermute(z[2], AXES, flipped(same))
    back_cross = lax.ppermute(z[3], AXES, flipped(cross))
    filtered = inverse_space(where, z[0], back_same, back_partner, back_cross, inverse, last)
    filtered = lax.all_to_all(filtered.reshape(256, 16, BLK), AXES, 0, 0, tiled=True)
    return unplane(filtered.reshape(shape))


def solution(mesh):
    return jax.shard_map(
        body,
        mesh=mesh,
        in_specs=(P(AXES, None), P(), P(None, "tile"), P()),
        out_specs=P(AXES, None),
        check_vma=False,
    )
```

```python
import functools

import jax
import jax.numpy as jnp
import numpy as np
from jax import lax
from jax.experimental import pallas as pl
from jax.experimental.pallas import tpu as pltpu
from jax.sharding import PartitionSpec as P
import ml_dtypes

K = 4096
ROOT = 64
WIN = 512
TAPS = 128
DEC = 4
BANDS = 8
HOP = 256
BINS = 256
BLK = 128
SLOTS = 32
HALF = 16
CHUNKS = 2
WIDTH = HALF // CHUNKS
PART = 2 * WIDTH
AXES = ("chan", "tile")
F32 = jnp.float32
BF16 = jnp.bfloat16
MIB = 1024 * 1024


def params(mib):
    return pltpu.CompilerParams(vmem_limit_bytes=mib * MIB)


VMEM = pl.BlockSpec(memory_space=pltpu.VMEM)
SMEM = pl.BlockSpec(memory_space=pltpu.SMEM)


def two(table):
    table = np.asarray(table, np.float32)
    hi = table.astype(ml_dtypes.bfloat16)
    lo = (table - hi.astype(np.float32)).astype(ml_dtypes.bfloat16)
    return hi, lo


def left_operand(table):
    hi, lo = two(table)
    return np.concatenate([hi, hi, lo], axis=-1)


def slot_order(core):
    width = HALF // CHUNKS
    order = []
    for g in range(CHUNKS):
        order += [(i + HALF * core) % SLOTS for i in range(g * width, (g + 1) * width)]
        order += [(i + HALF * (1 - core)) % SLOTS for i in range(g * width, (g + 1) * width)]
    return np.array(order)


def spatial_tables():
    c1 = np.arange(ROOT)
    slot = np.arange(SLOTS)[:, None]
    angle = 2 * np.pi / ROOT * (slot * c1 % ROOT)
    re, im = np.cos(angle), -np.sin(angle)
    im[0] = (-1.0) ** c1
    first = np.stack([re, im], axis=0)
    first = np.stack([first[:, slot_order(core)] for core in (0, 1)])
    first = first.reshape(2, 2, CHUNKS, SLOTS // CHUNKS, ROOT).swapaxes(1, 2).reshape(2, ROOT, ROOT)
    c0 = np.arange(ROOT)[None, :]
    k2 = np.arange(ROOT)[:, None]
    second = np.zeros((SLOTS, 2, ROOT, 2, ROOT))
    inverse = np.zeros((SLOTS, 2, ROOT, 2, ROOT))
    for s in range(SLOTS):
        phase = 2 * np.pi / K * ((s + ROOT * k2) * c0 % K)
        co, si = np.cos(phase), np.sin(phase)
        if s:
            second[s, 0, :, 0], second[s, 0, :, 1] = co, si
            second[s, 1, :, 0], second[s, 1, :, 1] = -si, co
            inverse[s, 0, :, 0], inverse[s, 0, :, 1] = co.T, -si.T
            inverse[s, 1, :, 0], inverse[s, 1, :, 1] = si.T, co.T
            continue
        n = ROOT // 2
        second[0, 0, :n, 0], second[0, 1, :n, 0] = co[:n], -si[:n]
        second[0, 1, 0, 0] = (-1.0) ** c0[0]
        inverse[0, 0, :, 0, :n], inverse[0, 0, :, 1, :n] = co[:n].T, -si[:n].T
        inverse[0, 0, :, 0, 0] = 0.5
        inverse[0, 0, :, 1, 0] = 0.5 * (-1.0) ** c0[0]
        phase = 2 * np.pi / K * ((n + ROOT * k2[:n]) * c0 % K)
        co, si = np.cos(phase), np.sin(phase)
        second[0, 0, n:, 1], second[0, 1, n:, 1] = co, -si
        inverse[0, 1, :, 0, n:], inverse[0, 1, :, 1, n:] = co.T, -si.T
    second = second.reshape(SLOTS, BLK, BLK)
    inverse = inverse.reshape(SLOTS, BLK, BLK) / K
    last = np.swapaxes(first, 1, 2)
    return (left_operand(first), left_operand(second), left_operand(inverse), left_operand(last))


def temporal_tables():
    s = np.arange(WIN)[:, None]
    f = np.arange(BINS)[None, :]
    angle = 2 * np.pi / WIN * (s * f % WIN)
    taper = np.sin(np.pi * (s + 0.5) / WIN)
    forward = np.concatenate([np.cos(angle), np.sin(angle)], axis=1) * taper
    weight = np.where(f == 0, 1.0, 2.0) / WIN
    backward = np.concatenate([np.cos(angle) * weight, np.sin(angle) * weight], axis=1) * taper
    return np.stack(two(forward)), np.stack(two(backward.T))


def chip_of(j):
    row, i = divmod(j, 4)
    z, q = divmod(row, 4)
    x = i if row % 2 == 0 else 3 - i
    y = q if z % 2 == 0 else 3 - q
    return x, y, z


def device_of(j, core):
    x, y, z = chip_of(j)
    return (((x // 2 * 4 + y) * 8 + z) * 2 + core) * 2 + x % 2


def permutes(windows):
    partner = [(device_of(j, c), device_of(j, 1 - c)) for j in range(windows) for c in (0, 1)]
    same, cross = [], []
    for j in range(windows - 1):
        same.append((device_of(j + 1, 0), device_of(j, 0)))
        same.append((device_of(j, 1), device_of(j + 1, 1)))
        cross.append((device_of(j + 1, 0), device_of(j, 1)))
        cross.append((device_of(j, 1), device_of(j + 1, 0)))
    return partner, same, cross


def flipped(pairs):
    return [(b, a) for a, b in pairs]


def split(value):
    hi = value.astype(BF16)
    return hi, (value - hi.astype(F32)).astype(BF16)


def stacked(value):
    hi, lo = split(value)
    return jnp.concatenate([hi, lo, hi], axis=0)


def dot(a, b):
    return jnp.dot(a, b, preferred_element_type=F32)


def plane_slot(b):
    j, core = divmod(b, 2)
    row, i = divmod(j, 4)
    x = i if row % 2 == 0 else 3 - i
    return x // 2, row, core, x % 2


def decimate_kernel(taps_ref, tail_ref, cur_ref, out_ref, band_ref):
    plane = pl.program_id(0)
    span = TAPS + DEC * BLK

    @pl.when(plane == 0)
    def _():
        i = lax.broadcasted_iota(jnp.int32, (TAPS, TAPS), 0)
        j = lax.broadcasted_iota(jnp.int32, (TAPS, TAPS), 1)
        mirror = (i + j == TAPS - 1).astype(BF16)
        rows = jnp.broadcast_to(taps_ref[...].astype(F32), (BLK, TAPS))
        mirrored = dot(rows.astype(BF16), mirror)
        wide = jnp.concatenate([mirrored, jnp.zeros((BLK, span - TAPS), F32)], axis=1)
        wide = pltpu.roll(wide, 1, 1, stride=DEC, stride_axis=0)
        band_ref[...] = wide.T.astype(BF16)

    tail = jnp.where(plane == 0, jnp.zeros_like(tail_ref[...]), tail_ref[...])
    blocks = cur_ref.shape[1] // (DEC * BLK)
    band = band_ref[...]
    group = 16
    for b0 in range(0, blocks, group):
        spans = []
        for b in range(b0, b0 + group):
            start = b * DEC * BLK
            if b == 0:
                spans.append(jnp.concatenate([tail, cur_ref[:, : DEC * BLK]], axis=1))
            else:
                spans.append(cur_ref[:, start - TAPS : start + DEC * BLK])
        result = dot(jnp.concatenate(spans, axis=0), band)
        for n in range(group):
            xh, row, core, xl = plane_slot(b0 + n)
            y = jnp.where(plane % 2 == 0, row, 3 - row)
            out_ref[xh, y, 0, core, xl] = result[n * 16 : (n + 1) * 16]


def decimate(raw, taps):
    channels, length = raw.shape
    planes = 8
    width = length // planes
    return pl.pallas_call(
        decimate_kernel,
        grid=(planes,),
        in_specs=[
            pl.BlockSpec((1, TAPS), lambda g: (0, 0)),
            pl.BlockSpec((channels, TAPS), lambda g: (0, jnp.maximum(g * (width // TAPS) - 1, 0))),
            pl.BlockSpec((channels, width), lambda g: (0, g)),
        ],
        out_specs=pl.BlockSpec((2, 4, 1, 2, 2, channels, BLK), lambda g: (0, 0, g, 0, 0, 0, 0)),
        out_shape=jax.ShapeDtypeStruct((2, 4, planes, 2, 2, channels, BLK), F32),
        scratch_shapes=[pltpu.VMEM((TAPS + DEC * BLK, BLK), BF16)],
        compiler_params=params(12),
        name="decimate",
    )(taps.reshape(1, TAPS), raw, raw)


def unplane_kernel(in_ref, out_ref):
    planes = in_ref.shape[2]
    for plane in range(planes):
        for b in range(32):
            xh, row, core, xl = plane_slot(b)
            y = row if plane % 2 == 0 else 3 - row
            start = (plane * 32 + b) * BLK
            out_ref[:, start : start + BLK] = in_ref[xh, y, plane, core, xl]


def unplane(blocks):
    planes = blocks.shape[2]
    channels = blocks.shape[5]
    return pl.pallas_call(
        unplane_kernel,
        in_specs=[VMEM],
        out_specs=VMEM,
        out_shape=jax.ShapeDtypeStruct((channels, planes * 32 * BLK), F32),
        compiler_params=params(8),
        name="unplane",
    )(blocks)


def real_slot(core, chunk, i):
    s = chunk * WIDTH + i % WIDTH + (HALF if i >= WIDTH else 0)
    return lax.rem(s + HALF * core, SLOTS)


def second_stage(core, chunk, mid_ref, second_ref, own_ref, other_ref):
    for i in range(PART):
        re = mid_ref[pl.ds(i, ROOT, stride=2 * PART), :]
        im = mid_ref[pl.ds(PART + i, ROOT, stride=2 * PART), :]
        table = second_ref[real_slot(core, chunk, i)]
        wave = dot(table, stacked(jnp.concatenate([re, im], axis=0)))
        if i < WIDTH:
            own_ref[i] = wave
        else:
            other_ref[i - WIDTH] = wave


def forward_kernel(where_ref, x_ref, first_ref, second_ref, own_ref, other_ref, *rest):
    later, mid_ref = rest[:-1], rest[-1]
    core = where_ref[0]
    first = first_ref[core]
    rows = 2 * PART
    for c0 in range(0, ROOT, 2):
        one = stacked(x_ref[pl.ds(c0, ROOT, stride=ROOT), :])
        two_ = stacked(x_ref[pl.ds(c0 + 1, ROOT, stride=ROOT), :])
        y = dot(first, jnp.concatenate([one, two_], axis=1))
        for g, ref in enumerate((mid_ref,) + later):
            ref[c0 * rows : (c0 + 1) * rows, :] = y[g * rows : (g + 1) * rows, :BLK]
            ref[(c0 + 1) * rows : (c0 + 2) * rows, :] = y[g * rows : (g + 1) * rows, BLK:]
    second_stage(core, 0, mid_ref, second_ref, own_ref, other_ref)


def forward_space(where, x, first, second):
    wave = jax.ShapeDtypeStruct((WIDTH, BLK, BLK), F32)
    middle = jax.ShapeDtypeStruct((K // CHUNKS, BLK), F32)
    return pl.pallas_call(
        forward_kernel,
        in_specs=[SMEM] + [VMEM] * 3,
        out_specs=[VMEM] * (1 + CHUNKS),
        out_shape=[wave] * 2 + [middle] * (CHUNKS - 1),
        scratch_shapes=[pltpu.VMEM((K // CHUNKS, BLK), F32)],
        compiler_params=params(14),
        name="forward_space",
    )(where, x, first, second)


def forward_more_kernel(chunk, where_ref, mid_ref, second_ref, own_ref, other_ref):
    second_stage(where_ref[0], chunk, mid_ref, second_ref, own_ref, other_ref)


def forward_more(chunk, where, middle, second):
    wave = jax.ShapeDtypeStruct((WIDTH, BLK, BLK), F32)
    return pl.pallas_call(
        functools.partial(forward_more_kernel, chunk),
        in_specs=[SMEM] + [VMEM] * 2,
        out_specs=[VMEM] * 2,
        out_shape=[wave] * 2,
        compiler_params=params(12),
        name="forward_more",
    )(where, middle, second)


def inverse_stage(core, chunk, own_ref, halo_ref, part_ref, cross_ref, inv_ref, mid_ref):
    for i in range(PART):
        if i < WIDTH:
            z = own_ref[i] + halo_ref[i]
        else:
            z = part_ref[i - WIDTH] + cross_ref[i - WIDTH]
        u = dot(inv_ref[real_slot(core, chunk, i)], stacked(z))
        mid_ref[pl.ds(i, ROOT, stride=2 * PART), :] = u[:ROOT]
        mid_ref[pl.ds(PART + i, ROOT, stride=2 * PART), :] = u[ROOT:]


def inverse_more_kernel(chunk, where_ref, own_ref, halo_ref, part_ref, cross_ref, inv_ref, mid_ref):
    inverse_stage(where_ref[0], chunk, own_ref, halo_ref, part_ref, cross_ref, inv_ref, mid_ref)


def inverse_more(chunk, where, waves, inv):
    return pl.pallas_call(
        functools.partial(inverse_more_kernel, chunk),
        in_specs=[SMEM] + [VMEM] * 5,
        out_specs=VMEM,
        out_shape=jax.ShapeDtypeStruct((K // CHUNKS, BLK), F32),
        compiler_params=params(12),
        name="inverse_more",
    )(where, *waves, inv)


def inverse_kernel(where_ref, own_ref, halo_ref, part_ref, cross_ref, inv_ref, last_ref, *rest):
    earlier, out_ref, mid_ref = rest[:-2], rest[-2], rest[-1]
    core = where_ref[0]
    inverse_stage(core, CHUNKS - 1, own_ref, halo_ref, part_ref, cross_ref, inv_ref, mid_ref)
    last = last_ref[core]
    rows = 2 * PART
    refs = earlier + (mid_ref,)

    def column(c0):
        return stacked(jnp.concatenate([ref[c0 * rows : (c0 + 1) * rows, :] for ref in refs], axis=0))

    for c0 in range(0, ROOT, 2):
        y = dot(last, jnp.concatenate([column(c0), column(c0 + 1)], axis=1))
        out_ref[pl.ds(c0, ROOT, stride=ROOT), :] = y[:, :BLK]
        out_ref[pl.ds(c0 + 1, ROOT, stride=ROOT), :] = y[:, BLK:]


def inverse_space(where, waves, earlier, inv, last):
    return pl.pallas_call(
        inverse_kernel,
        in_specs=[SMEM] + [VMEM] * (6 + len(earlier)),
        out_specs=VMEM,
        out_shape=jax.ShapeDtypeStruct((K, BLK), F32),
        scratch_shapes=[pltpu.VMEM((K // CHUNKS, BLK), F32)],
        compiler_params=params(14),
        name="inverse_space",
    )(where, *waves, inv, last, *earlier)


def gains_kernel(where_ref, gain_ref, band_ref, out_ref):
    core = where_ref[0]
    n = ROOT // 2
    i = lax.broadcasted_iota(jnp.int32, (ROOT, ROOT), 0)
    j = lax.broadcasted_iota(jnp.int32, (ROOT, ROOT), 1)
    mirror = (i + j == ROOT - 1).astype(BF16)
    source = jnp.where(i == 0, 0, jnp.where(i < n, n - i, n + ROOT - 1 - i))
    mirror0 = (j == source).astype(BF16)

    def rows(k1, k2, count):
        return band_ref[pl.ds(k1 + ROOT * k2, count, stride=ROOT), :]

    def exact(perm, bands):
        return dot(perm, bands.astype(F32).astype(BF16))

    def pick(bands):
        total = jnp.zeros(bands.shape, F32)
        for b in range(BANDS):
            total = jnp.where(bands == b, gain_ref[b], total)
        return total

    def put(s, plus, minus):
        gp, gm = pick(plus.astype(F32)), pick(minus)
        out_ref[0, s] = gp + gm
        out_ref[1, s] = gp - gm

    for s in range(HALF):
        if s:
            k1 = s + HALF * core
            put(s, rows(k1, 0, ROOT), exact(mirror, rows(ROOT - k1, 0, ROOT)))
            continue

        @pl.when(core == 0)
        def _():
            plus = jnp.concatenate([rows(0, 0, n), rows(n, 0, n)], axis=0)
            minus = jnp.concatenate([rows(0, n, n), rows(n, n, n)], axis=0)
            put(0, plus, exact(mirror0, minus))

        @pl.when(core != 0)
        def _():
            put(0, rows(HALF, 0, ROOT), exact(mirror, rows(ROOT - HALF, 0, ROOT)))


def gains(where, band_gain, fan_band):
    return pl.pallas_call(
        gains_kernel,
        in_specs=[SMEM] * 2 + [VMEM],
        out_specs=VMEM,
        out_shape=jax.ShapeDtypeStruct((2, HALF, ROOT, BLK), F32),
        compiler_params=params(8),
        name="gains",
    )(where, band_gain, fan_band)


def time_kernel(first_chunk, where_ref, *refs):
    own_ref, part_ref, same_ref, cross_ref, mine_ref, theirs_ref, fwd_ref, bwd_ref = refs[:8]
    out_refs = refs[8:]
    core, xl = where_ref[0], where_ref[1]
    step = pl.program_id(0)
    slots = own_ref.shape[0]
    rows = slots * BLK
    even = core == 0

    def flat(ref):
        return ref[...].reshape(rows, BLK)

    own, part, same, cross = flat(own_ref), flat(part_ref), flat(same_ref), flat(cross_ref)
    x = jnp.concatenate(
        [
            jnp.where(even, cross, same),
            jnp.where(even, own, part),
            jnp.where(even, part, own),
            jnp.where(even, same, cross),
        ],
        axis=1,
    )
    hi, lo = split(x)
    fwd_hi = fwd_ref[0]
    v = dot(hi, fwd_hi) + dot(lo, fwd_hi) + dot(hi, fwd_ref[1])
    pieces = []
    for s in range(slots):
        p = v[s * BLK : s * BLK + ROOT]
        q = v[s * BLK + ROOT : (s + 1) * BLK]
        a, d = p[:, :BINS], p[:, BINS:]
        c, b = q[:, :BINS], q[:, BINS:]

        def wide(kind):
            mine, theirs = mine_ref[kind, s], theirs_ref[kind, s]
            low = jnp.where(xl == 0, mine, theirs)
            high = jnp.where(xl == 0, theirs, mine)
            return jnp.concatenate([low, high], axis=1)

        gs, gd = wide(0), wide(1)
        gr = gi = gs
        if s == 0 and first_chunk:
            row = lax.broadcasted_iota(jnp.int32, (ROOT, BINS), 0)
            pair = (row == 0) & (step == 0) & even
            gr = jnp.where(pair, gs + gd, gs)
            gi = jnp.where(pair, gs - gd, gs)
            gd = jnp.where(pair, 0.0, gd)
        pieces.append(jnp.concatenate([gr * a + gd * b, gr * d - gd * c], axis=1))
        pieces.append(jnp.concatenate([gi * c - gd * d, gd * a + gi * b], axis=1))
    hi, lo = split(jnp.concatenate(pieces, axis=0))
    bwd_hi = bwd_ref[0]
    z = dot(hi, bwd_hi) + dot(lo, bwd_hi) + dot(hi, bwd_ref[1])
    before, low, high, after = (z[:, n * BLK : (n + 1) * BLK] for n in range(4))
    outs = [
        jnp.where(even, low, high),
        jnp.where(even, high, low),
        jnp.where(even, after, before),
        jnp.where(even, before, after),
    ]
    for out_ref, value in zip(out_refs, outs):
        out_ref[...] = value.reshape(slots, BLK, BLK)


def time_filter(chunk, where, waves, mine, theirs, fwd, bwd):
    slots = 4
    steps = WIDTH // slots
    data = pl.BlockSpec((slots, BLK, BLK), lambda g: (g, 0, 0))
    gain = pl.BlockSpec((2, slots, ROOT, BLK), lambda g: (0, chunk * steps + g, 0, 0))
    table = pl.BlockSpec((2, WIN, WIN), lambda g: (0, 0, 0))
    return pl.pallas_call(
        functools.partial(time_kernel, chunk == 0),
        grid=(steps,),
        in_specs=[SMEM] + [data] * 4 + [gain] * 2 + [table] * 2,
        out_specs=[data] * 4,
        out_shape=[jax.ShapeDtypeStruct((WIDTH, BLK, BLK), F32)] * 4,
        compiler_params=params(24),
        name="time_filter",
    )(where, *waves, mine, theirs, fwd, bwd)


def body(raw_strain, fir_taps, fan_band, band_gain):
    where = jnp.stack([lax.axis_index("chan") % 2, lax.axis_index("tile")]).astype(jnp.int32)
    first, second, inverse, last = (jnp.asarray(t) for t in spatial_tables())
    fwd, bwd = (jnp.asarray(t) for t in temporal_tables())
    partner, same, cross = permutes(raw_strain.shape[1] // DEC // HOP)

    mine = gains(where, band_gain, fan_band)
    theirs = lax.ppermute(mine, "tile", [(0, 1), (1, 0)])

    blocks = decimate(raw_strain, fir_taps)
    shape = blocks.shape
    blocks = blocks.reshape((256,) + shape[5:])
    blocks = lax.all_to_all(blocks, AXES, 0, 0, tiled=True)
    own, other, *middle = forward_space(where, blocks.reshape(K, BLK), first, second)
    received = []
    for g in range(CHUNKS):
        if g:
            own, other = forward_more(g, where, middle[g - 1], second)
        from_partner = lax.ppermute(other, AXES, partner)
        from_same = lax.ppermute(own, AXES, same)
        from_cross = lax.ppermute(other, AXES, cross)
        received.append((own, from_partner, from_same, from_cross))
    returned = []
    for g in range(CHUNKS):
        own, part, halo, far = time_filter(g, where, received[g], mine, theirs, fwd, bwd)
        back_partner = lax.ppermute(part, AXES, partner)
        back_same = lax.ppermute(halo, AXES, flipped(same))
        back_cross = lax.ppermute(far, AXES, flipped(cross))
        returned.append((own, back_same, back_partner, back_cross))
    earlier = [inverse_more(g, where, returned[g], inverse) for g in range(CHUNKS - 1)]
    filtered = inverse_space(where, returned[-1], earlier, inverse, last)
    filtered = lax.all_to_all(filtered.reshape(256, 16, BLK), AXES, 0, 0, tiled=True)
    return unplane(filtered.reshape(shape))


def solution(mesh):
    return jax.shard_map(
        body,
        mesh=mesh,
        in_specs=(P(AXES, None), P(), P(None, "tile"), P()),
        out_specs=P(AXES, None),
        check_vma=False,
    )
```

```python
import functools

import jax
import jax.numpy as jnp
import numpy as np
from jax import lax
from jax.experimental import pallas as pl
from jax.experimental.pallas import tpu as pltpu
from jax.sharding import PartitionSpec as P
import ml_dtypes

K = 4096
ROOT = 64
WIN = 512
TAPS = 128
DEC = 4
BANDS = 8
HOP = 256
BINS = 256
BLK = 128
SLOTS = 32
HALF = 16
CHUNKS = 2
WIDTH = HALF // CHUNKS
PART = 2 * WIDTH
AXES = ("chan", "tile")
F32 = jnp.float32
BF16 = jnp.bfloat16
MIB = 1024 * 1024


def params(mib):
    return pltpu.CompilerParams(vmem_limit_bytes=mib * MIB)


VMEM = pl.BlockSpec(memory_space=pltpu.VMEM)
SMEM = pl.BlockSpec(memory_space=pltpu.SMEM)
ANY = pl.BlockSpec(memory_space=pl.ANY)


def two(table):
    table = np.asarray(table, np.float32)
    hi = table.astype(ml_dtypes.bfloat16)
    lo = (table - hi.astype(np.float32)).astype(ml_dtypes.bfloat16)
    return hi, lo


def left_operand(table):
    hi, lo = two(table)
    return np.concatenate([hi, hi, lo], axis=-1)


def slot_order(core):
    width = HALF // CHUNKS
    order = []
    for g in range(CHUNKS):
        order += [(i + HALF * core) % SLOTS for i in range(g * width, (g + 1) * width)]
        order += [(i + HALF * (1 - core)) % SLOTS for i in range(g * width, (g + 1) * width)]
    return np.array(order)


def spatial_tables():
    c1 = np.arange(ROOT)
    slot = np.arange(SLOTS)[:, None]
    angle = 2 * np.pi / ROOT * (slot * c1 % ROOT)
    re, im = np.cos(angle), -np.sin(angle)
    im[0] = (-1.0) ** c1
    first = np.stack([re, im], axis=0)
    first = np.stack([first[:, slot_order(core)] for core in (0, 1)])
    first = first.reshape(2, 2, CHUNKS, SLOTS // CHUNKS, ROOT).swapaxes(1, 2).reshape(2, ROOT, ROOT)
    c0 = np.arange(ROOT)[None, :]
    k2 = np.arange(ROOT)[:, None]
    second = np.zeros((SLOTS, 2, ROOT, 2, ROOT))
    inverse = np.zeros((SLOTS, 2, ROOT, 2, ROOT))
    for s in range(SLOTS):
        phase = 2 * np.pi / K * ((s + ROOT * k2) * c0 % K)
        co, si = np.cos(phase), np.sin(phase)
        if s:
            second[s, 0, :, 0], second[s, 0, :, 1] = co, si
            second[s, 1, :, 0], second[s, 1, :, 1] = -si, co
            inverse[s, 0, :, 0], inverse[s, 0, :, 1] = co.T, -si.T
            inverse[s, 1, :, 0], inverse[s, 1, :, 1] = si.T, co.T
            continue
        n = ROOT // 2
        second[0, 0, :n, 0], second[0, 1, :n, 0] = co[:n], -si[:n]
        second[0, 1, 0, 0] = (-1.0) ** c0[0]
        inverse[0, 0, :, 0, :n], inverse[0, 0, :, 1, :n] = co[:n].T, -si[:n].T
        inverse[0, 0, :, 0, 0] = 0.5
        inverse[0, 0, :, 1, 0] = 0.5 * (-1.0) ** c0[0]
        phase = 2 * np.pi / K * ((n + ROOT * k2[:n]) * c0 % K)
        co, si = np.cos(phase), np.sin(phase)
        second[0, 0, n:, 1], second[0, 1, n:, 1] = co, -si
        inverse[0, 1, :, 0, n:], inverse[0, 1, :, 1, n:] = co.T, -si.T
    second = second.reshape(SLOTS, BLK, BLK)
    inverse = inverse.reshape(SLOTS, BLK, BLK) / K
    last = np.swapaxes(first, 1, 2)
    return (left_operand(first), left_operand(second), left_operand(inverse), left_operand(last))


def temporal_tables():
    s = np.arange(WIN)[:, None]
    f = np.arange(BINS)[None, :]
    angle = 2 * np.pi / WIN * (s * f % WIN)
    taper = np.sin(np.pi * (s + 0.5) / WIN)
    forward = np.concatenate([np.cos(angle), np.sin(angle)], axis=1) * taper
    weight = np.where(f == 0, 1.0, 2.0) / WIN
    backward = np.concatenate([np.cos(angle) * weight, np.sin(angle) * weight], axis=1) * taper
    return np.stack(two(forward)), np.stack(two(backward.T))


def chip_of(j):
    row, i = divmod(j, 4)
    z, q = divmod(row, 4)
    x = i if row % 2 == 0 else 3 - i
    y = q if z % 2 == 0 else 3 - q
    return x, y, z


def device_of(j, core):
    x, y, z = chip_of(j)
    return (((x // 2 * 4 + y) * 8 + z) * 2 + core) * 2 + x % 2


def permutes(windows):
    partner = [(device_of(j, c), device_of(j, 1 - c)) for j in range(windows) for c in (0, 1)]
    same, cross = [], []
    for j in range(windows - 1):
        same.append((device_of(j + 1, 0), device_of(j, 0)))
        same.append((device_of(j, 1), device_of(j + 1, 1)))
        cross.append((device_of(j + 1, 0), device_of(j, 1)))
        cross.append((device_of(j, 1), device_of(j + 1, 0)))
    return partner, same, cross


def flipped(pairs):
    return [(b, a) for a, b in pairs]


def split(value):
    hi = value.astype(BF16)
    return hi, (value - hi.astype(F32)).astype(BF16)


def stacked(value):
    hi, lo = split(value)
    return jnp.concatenate([hi, lo, hi], axis=0)


def dot(a, b):
    return jnp.dot(a, b, preferred_element_type=F32)


def plane_slot(b):
    j, core = divmod(b, 2)
    row, i = divmod(j, 4)
    x = i if row % 2 == 0 else 3 - i
    return x // 2, row, core, x % 2


def decimate_kernel(taps_ref, raw_ref, out_ref, cur_ref, band_ref, stage_ref, in_sems, out_sems):
    planes = out_ref.shape[2]
    span = TAPS + DEC * BLK
    width = raw_ref.shape[1] // planes
    loads = []
    for plane in range(planes):
        part = pl.ds(plane * width, width)
        loads.append(pltpu.make_async_copy(raw_ref.at[:, part], cur_ref.at[:, part], in_sems.at[plane]))
        loads[-1].start()

    i = lax.broadcasted_iota(jnp.int32, (TAPS, TAPS), 0)
    j = lax.broadcasted_iota(jnp.int32, (TAPS, TAPS), 1)
    mirror = (i + j == TAPS - 1).astype(BF16)
    rows = jnp.broadcast_to(taps_ref[...].astype(F32), (BLK, TAPS))
    mirrored = dot(rows.astype(BF16), mirror)
    wide = jnp.concatenate([mirrored, jnp.zeros((BLK, span - TAPS), F32)], axis=1)
    wide = pltpu.roll(wide, 1, 1, stride=DEC, stride_axis=0)
    band_ref[...] = wide.T.astype(BF16)

    blocks = width // (DEC * BLK)
    group = 16
    band = band_ref[...]
    stores = []
    for plane in range(planes):
        loads[plane].wait()
        for b0 in range(0, blocks, group):
            spans = []
            for b in range(b0, b0 + group):
                start = plane * width + b * DEC * BLK
                if start == 0:
                    tail = jnp.zeros((cur_ref.shape[0], TAPS), BF16)
                    spans.append(jnp.concatenate([tail, cur_ref[:, : DEC * BLK]], axis=1))
                else:
                    spans.append(cur_ref[:, start - TAPS : start + DEC * BLK])
            result = dot(jnp.concatenate(spans, axis=0), band)
            for n in range(group):
                xh, row, core, xl = plane_slot(b0 + n)
                y = row if plane % 2 == 0 else 3 - row
                stage_ref[plane, xh, y, core, xl] = result[n * 16 : (n + 1) * 16]
        stores.append(pltpu.make_async_copy(stage_ref.at[plane], out_ref.at[:, :, plane], out_sems.at[plane]))
        stores[-1].start()
    for store in stores:
        store.wait()


def decimate(raw, taps):
    channels, length = raw.shape
    planes = 8
    return pl.pallas_call(
        decimate_kernel,
        in_specs=[VMEM, ANY],
        out_specs=ANY,
        out_shape=jax.ShapeDtypeStruct((2, 4, planes, 2, 2, channels, BLK), F32),
        scratch_shapes=[
            pltpu.VMEM(raw.shape, BF16),
            pltpu.VMEM((TAPS + DEC * BLK, BLK), BF16),
            pltpu.VMEM((planes, 2, 4, 2, 2, channels, BLK), F32),
            pltpu.SemaphoreType.DMA((planes,)),
            pltpu.SemaphoreType.DMA((planes,)),
        ],
        compiler_params=params(60),
        name="decimate",
    )(taps.reshape(1, TAPS), raw)


def unplane_kernel(in_ref, out_ref):
    planes = in_ref.shape[2]
    for plane in range(planes):
        for b in range(32):
            xh, row, core, xl = plane_slot(b)
            y = row if plane % 2 == 0 else 3 - row
            start = (plane * 32 + b) * BLK
            out_ref[:, start : start + BLK] = in_ref[xh, y, plane, core, xl]


def unplane(blocks):
    planes = blocks.shape[2]
    channels = blocks.shape[5]
    return pl.pallas_call(
        unplane_kernel,
        in_specs=[VMEM],
        out_specs=VMEM,
        out_shape=jax.ShapeDtypeStruct((channels, planes * 32 * BLK), F32),
        compiler_params=params(8),
        name="unplane",
    )(blocks)


def real_slot(core, chunk, i):
    s = chunk * WIDTH + i % WIDTH + (HALF if i >= WIDTH else 0)
    return lax.rem(s + HALF * core, SLOTS)


def second_stage(core, chunk, mid_ref, second_ref, own_ref, other_ref):
    for i in range(PART):
        re = mid_ref[pl.ds(i, ROOT, stride=2 * PART), :]
        im = mid_ref[pl.ds(PART + i, ROOT, stride=2 * PART), :]
        table = second_ref[real_slot(core, chunk, i)]
        wave = dot(table, stacked(jnp.concatenate([re, im], axis=0)))
        if i < WIDTH:
            own_ref[i] = wave
        else:
            other_ref[i - WIDTH] = wave


def forward_kernel(where_ref, x_ref, first_ref, second_ref, own_ref, other_ref, *rest):
    later, mid_ref = rest[:-1], rest[-1]
    core = where_ref[0]
    first = first_ref[core]
    rows = 2 * PART
    for c0 in range(0, ROOT, 2):
        one = stacked(x_ref[pl.ds(c0, ROOT, stride=ROOT), :])
        two_ = stacked(x_ref[pl.ds(c0 + 1, ROOT, stride=ROOT), :])
        y = dot(first, jnp.concatenate([one, two_], axis=1))
        for g, ref in enumerate((mid_ref,) + later):
            ref[c0 * rows : (c0 + 1) * rows, :] = y[g * rows : (g + 1) * rows, :BLK]
            ref[(c0 + 1) * rows : (c0 + 2) * rows, :] = y[g * rows : (g + 1) * rows, BLK:]
    second_stage(core, 0, mid_ref, second_ref, own_ref, other_ref)


def forward_space(where, x, first, second):
    wave = jax.ShapeDtypeStruct((WIDTH, BLK, BLK), F32)
    middle = jax.ShapeDtypeStruct((K // CHUNKS, BLK), F32)
    return pl.pallas_call(
        forward_kernel,
        in_specs=[SMEM] + [VMEM] * 3,
        out_specs=[VMEM] * (1 + CHUNKS),
        out_shape=[wave] * 2 + [middle] * (CHUNKS - 1),
        scratch_shapes=[pltpu.VMEM((K // CHUNKS, BLK), F32)],
        compiler_params=params(14),
        name="forward_space",
    )(where, x, first, second)


def forward_more_kernel(chunk, where_ref, mid_ref, second_ref, own_ref, other_ref):
    second_stage(where_ref[0], chunk, mid_ref, second_ref, own_ref, other_ref)


def forward_more(chunk, where, middle, second):
    wave = jax.ShapeDtypeStruct((WIDTH, BLK, BLK), F32)
    return pl.pallas_call(
        functools.partial(forward_more_kernel, chunk),
        in_specs=[SMEM] + [VMEM] * 2,
        out_specs=[VMEM] * 2,
        out_shape=[wave] * 2,
        compiler_params=params(12),
        name="forward_more",
    )(where, middle, second)


def inverse_stage(core, chunk, own_ref, halo_ref, part_ref, cross_ref, inv_ref, mid_ref):
    for i in range(PART):
        if i < WIDTH:
            z = own_ref[i] + halo_ref[i]
        else:
            z = part_ref[i - WIDTH] + cross_ref[i - WIDTH]
        u = dot(inv_ref[real_slot(core, chunk, i)], stacked(z))
        mid_ref[pl.ds(i, ROOT, stride=2 * PART), :] = u[:ROOT]
        mid_ref[pl.ds(PART + i, ROOT, stride=2 * PART), :] = u[ROOT:]


def inverse_more_kernel(chunk, where_ref, own_ref, halo_ref, part_ref, cross_ref, inv_ref, mid_ref):
    inverse_stage(where_ref[0], chunk, own_ref, halo_ref, part_ref, cross_ref, inv_ref, mid_ref)


def inverse_more(chunk, where, waves, inv):
    return pl.pallas_call(
        functools.partial(inverse_more_kernel, chunk),
        in_specs=[SMEM] + [VMEM] * 5,
        out_specs=VMEM,
        out_shape=jax.ShapeDtypeStruct((K // CHUNKS, BLK), F32),
        compiler_params=params(12),
        name="inverse_more",
    )(where, *waves, inv)


def inverse_kernel(where_ref, own_ref, halo_ref, part_ref, cross_ref, inv_ref, last_ref, *rest):
    earlier, out_ref, mid_ref = rest[:-2], rest[-2], rest[-1]
    core = where_ref[0]
    inverse_stage(core, CHUNKS - 1, own_ref, halo_ref, part_ref, cross_ref, inv_ref, mid_ref)
    last = last_ref[core]
    rows = 2 * PART
    refs = earlier + (mid_ref,)

    def column(c0):
        return stacked(jnp.concatenate([ref[c0 * rows : (c0 + 1) * rows, :] for ref in refs], axis=0))

    for c0 in range(0, ROOT, 2):
        y = dot(last, jnp.concatenate([column(c0), column(c0 + 1)], axis=1))
        out_ref[pl.ds(c0, ROOT, stride=ROOT), :] = y[:, :BLK]
        out_ref[pl.ds(c0 + 1, ROOT, stride=ROOT), :] = y[:, BLK:]


def inverse_space(where, waves, earlier, inv, last):
    return pl.pallas_call(
        inverse_kernel,
        in_specs=[SMEM] + [VMEM] * (6 + len(earlier)),
        out_specs=VMEM,
        out_shape=jax.ShapeDtypeStruct((K, BLK), F32),
        scratch_shapes=[pltpu.VMEM((K // CHUNKS, BLK), F32)],
        compiler_params=params(14),
        name="inverse_space",
    )(where, *waves, inv, last, *earlier)


def gains_kernel(where_ref, gain_ref, band_ref, out_ref):
    core = where_ref[0]
    n = ROOT // 2
    i = lax.broadcasted_iota(jnp.int32, (ROOT, ROOT), 0)
    j = lax.broadcasted_iota(jnp.int32, (ROOT, ROOT), 1)
    mirror = (i + j == ROOT - 1).astype(BF16)
    source = jnp.where(i == 0, 0, jnp.where(i < n, n - i, n + ROOT - 1 - i))
    mirror0 = (j == source).astype(BF16)

    def rows(k1, k2, count):
        return band_ref[pl.ds(k1 + ROOT * k2, count, stride=ROOT), :]

    def exact(perm, bands):
        return dot(perm, bands.astype(F32).astype(BF16))

    def pick(bands):
        total = jnp.zeros(bands.shape, F32)
        for b in range(BANDS):
            total = jnp.where(bands == b, gain_ref[b], total)
        return total

    def put(s, plus, minus):
        gp, gm = pick(plus.astype(F32)), pick(minus)
        out_ref[0, s] = gp + gm
        out_ref[1, s] = gp - gm

    for s in range(HALF):
        if s:
            k1 = s + HALF * core
            put(s, rows(k1, 0, ROOT), exact(mirror, rows(ROOT - k1, 0, ROOT)))
            continue

        @pl.when(core == 0)
        def _():
            plus = jnp.concatenate([rows(0, 0, n), rows(n, 0, n)], axis=0)
            minus = jnp.concatenate([rows(0, n, n), rows(n, n, n)], axis=0)
            put(0, plus, exact(mirror0, minus))

        @pl.when(core != 0)
        def _():
            put(0, rows(HALF, 0, ROOT), exact(mirror, rows(ROOT - HALF, 0, ROOT)))


def gains(where, band_gain, fan_band):
    return pl.pallas_call(
        gains_kernel,
        in_specs=[SMEM] * 2 + [VMEM],
        out_specs=VMEM,
        out_shape=jax.ShapeDtypeStruct((2, HALF, ROOT, BLK), F32),
        compiler_params=params(8),
        name="gains",
    )(where, band_gain, fan_band)


def time_kernel(first_chunk, where_ref, *refs):
    own_ref, part_ref, same_ref, cross_ref, mine_ref, theirs_ref, fwd_ref, bwd_ref = refs[:8]
    out_refs = refs[8:]
    core, xl = where_ref[0], where_ref[1]
    step = pl.program_id(0)
    slots = own_ref.shape[0]
    rows = slots * BLK
    even = core == 0

    def flat(ref):
        return ref[...].reshape(rows, BLK)

    own, part, same, cross = flat(own_ref), flat(part_ref), flat(same_ref), flat(cross_ref)
    x = jnp.concatenate(
        [
            jnp.where(even, cross, same),
            jnp.where(even, own, part),
            jnp.where(even, part, own),
            jnp.where(even, same, cross),
        ],
        axis=1,
    )
    hi, lo = split(x)
    fwd_hi = fwd_ref[0]
    v = dot(hi, fwd_hi) + dot(lo, fwd_hi) + dot(hi, fwd_ref[1])
    pieces = []
    for s in range(slots):
        p = v[s * BLK : s * BLK + ROOT]
        q = v[s * BLK + ROOT : (s + 1) * BLK]
        a, d = p[:, :BINS], p[:, BINS:]
        c, b = q[:, :BINS], q[:, BINS:]

        def wide(kind):
            mine, theirs = mine_ref[kind, s], theirs_ref[kind, s]
            low = jnp.where(xl == 0, mine, theirs)
            high = jnp.where(xl == 0, theirs, mine)
            return jnp.concatenate([low, high], axis=1)

        gs, gd = wide(0), wide(1)
        gr = gi = gs
        if s == 0 and first_chunk:
            row = lax.broadcasted_iota(jnp.int32, (ROOT, BINS), 0)
            pair = (row == 0) & (step == 0) & even
            gr = jnp.where(pair, gs + gd, gs)
            gi = jnp.where(pair, gs - gd, gs)
            gd = jnp.where(pair, 0.0, gd)
        pieces.append(jnp.concatenate([gr * a + gd * b, gr * d - gd * c], axis=1))
        pieces.append(jnp.concatenate([gi * c - gd * d, gd * a + gi * b], axis=1))
    hi, lo = split(jnp.concatenate(pieces, axis=0))
    bwd_hi = bwd_ref[0]
    z = dot(hi, bwd_hi) + dot(lo, bwd_hi) + dot(hi, bwd_ref[1])
    before, low, high, after = (z[:, n * BLK : (n + 1) * BLK] for n in range(4))
    outs = [
        jnp.where(even, low, high),
        jnp.where(even, high, low),
        jnp.where(even, after, before),
        jnp.where(even, before, after),
    ]
    for out_ref, value in zip(out_refs, outs):
        out_ref[...] = value.reshape(slots, BLK, BLK)


def time_filter(chunk, where, waves, mine, theirs, fwd, bwd):
    slots = 4
    steps = WIDTH // slots
    data = pl.BlockSpec((slots, BLK, BLK), lambda g: (g, 0, 0))
    gain = pl.BlockSpec((2, slots, ROOT, BLK), lambda g: (0, chunk * steps + g, 0, 0))
    table = pl.BlockSpec((2, WIN, WIN), lambda g: (0, 0, 0))
    return pl.pallas_call(
        functools.partial(time_kernel, chunk == 0),
        grid=(steps,),
        in_specs=[SMEM] + [data] * 4 + [gain] * 2 + [table] * 2,
        out_specs=[data] * 4,
        out_shape=[jax.ShapeDtypeStruct((WIDTH, BLK, BLK), F32)] * 4,
        compiler_params=params(24),
        name="time_filter",
    )(where, *waves, mine, theirs, fwd, bwd)


def body(raw_strain, fir_taps, fan_band, band_gain):
    where = jnp.stack([lax.axis_index("chan") % 2, lax.axis_index("tile")]).astype(jnp.int32)
    first, second, inverse, last = (jnp.asarray(t) for t in spatial_tables())
    fwd, bwd = (jnp.asarray(t) for t in temporal_tables())
    partner, same, cross = permutes(raw_strain.shape[1] // DEC // HOP)

    mine = gains(where, band_gain, fan_band)
    theirs = lax.ppermute(mine, "tile", [(0, 1), (1, 0)])

    blocks = decimate(raw_strain, fir_taps)
    shape = blocks.shape
    blocks = blocks.reshape((256,) + shape[5:])
    blocks = lax.all_to_all(blocks, AXES, 0, 0, tiled=True)
    own, other, *middle = forward_space(where, blocks.reshape(K, BLK), first, second)
    received = []
    for g in range(CHUNKS):
        if g:
            own, other = forward_more(g, where, middle[g - 1], second)
        from_partner = lax.ppermute(other, AXES, partner)
        from_same = lax.ppermute(own, AXES, same)
        from_cross = lax.ppermute(other, AXES, cross)
        received.append((own, from_partner, from_same, from_cross))
    returned = []
    for g in range(CHUNKS):
        own, part, halo, far = time_filter(g, where, received[g], mine, theirs, fwd, bwd)
        back_partner = lax.ppermute(part, AXES, partner)
        back_same = lax.ppermute(halo, AXES, flipped(same))
        back_cross = lax.ppermute(far, AXES, flipped(cross))
        returned.append((own, back_same, back_partner, back_cross))
    earlier = [inverse_more(g, where, returned[g], inverse) for g in range(CHUNKS - 1)]
    filtered = inverse_space(where, returned[-1], earlier, inverse, last)
    filtered = lax.all_to_all(filtered.reshape(256, 16, BLK), AXES, 0, 0, tiled=True)
    return unplane(filtered.reshape(shape))


def solution(mesh):
    return jax.shard_map(
        body,
        mesh=mesh,
        in_specs=(P(AXES, None), P(), P(None, "tile"), P()),
        out_specs=P(AXES, None),
        check_vma=False,
    )
```

```python
import functools

import jax
import jax.numpy as jnp
import numpy as np
from jax import lax
from jax.experimental import pallas as pl
from jax.experimental.pallas import tpu as pltpu
from jax.sharding import PartitionSpec as P
import ml_dtypes

K = 4096
ROOT = 64
WIN = 512
TAPS = 128
DEC = 4
BANDS = 8
HOP = 256
BINS = 256
BLK = 128
SLOTS = 32
HALF = 16
CHUNKS = 2
WIDTH = HALF // CHUNKS
PART = 2 * WIDTH
AXES = ("chan", "tile")
F32 = jnp.float32
BF16 = jnp.bfloat16
MIB = 1024 * 1024
WAVE = jax.ShapeDtypeStruct((WIDTH, BLK, BLK), F32)
MIDDLE = jax.ShapeDtypeStruct((PART, BLK, BLK), F32)


def params(mib):
    return pltpu.CompilerParams(vmem_limit_bytes=mib * MIB)


VMEM = pl.BlockSpec(memory_space=pltpu.VMEM)
SMEM = pl.BlockSpec(memory_space=pltpu.SMEM)
ANY = pl.BlockSpec(memory_space=pl.ANY)


def two(table):
    table = np.asarray(table, np.float32)
    hi = table.astype(ml_dtypes.bfloat16)
    lo = (table - hi.astype(np.float32)).astype(ml_dtypes.bfloat16)
    return hi, lo


def left_operand(table):
    hi, lo = two(table)
    return np.concatenate([hi, hi, lo], axis=-1)


def spatial_tables():
    c0 = np.arange(ROOT)[None, :]
    k2 = np.arange(ROOT)[:, None]
    second = np.zeros((SLOTS, 2, ROOT, 2, ROOT))
    inverse = np.zeros((SLOTS, 2, ROOT, 2, ROOT))
    for s in range(SLOTS):
        phase = 2 * np.pi / K * ((s + ROOT * k2) * c0 % K)
        co, si = np.cos(phase), np.sin(phase)
        if s:
            second[s, 0, :, 0], second[s, 0, :, 1] = co, si
            second[s, 1, :, 0], second[s, 1, :, 1] = -si, co
            inverse[s, 0, :, 0], inverse[s, 0, :, 1] = co.T / 2, -si.T / 2
            inverse[s, 1, :, 0], inverse[s, 1, :, 1] = si.T / 2, co.T / 2
            continue
        n = ROOT // 2
        second[0, 0, :n, 0], second[0, 1, :n, 0] = co[:n], -si[:n]
        second[0, 1, 0, 0] = (-1.0) ** c0[0]
        inverse[0, 0, :, 0, :n], inverse[0, 0, :, 1, :n] = co[:n].T, -si[:n].T
        inverse[0, 0, :, 0, 0] = 0.5
        inverse[0, 0, :, 1, 0] = 0.5 * (-1.0) ** c0[0]
        phase = 2 * np.pi / K * ((n + ROOT * k2[:n]) * c0 % K)
        co, si = np.cos(phase), np.sin(phase)
        second[0, 0, n:, 1], second[0, 1, n:, 1] = co, -si
        inverse[0, 1, :, 0, n:], inverse[0, 1, :, 1, n:] = co.T, -si.T
    second = second.reshape(SLOTS, BLK, BLK)
    inverse = inverse.reshape(SLOTS, BLK, BLK) / K
    return left_operand(second), left_operand(inverse)


def temporal_tables():
    s = np.arange(WIN)[:, None]
    f = np.arange(BINS)[None, :]
    angle = 2 * np.pi / WIN * (s * f % WIN)
    taper = np.sin(np.pi * (s + 0.5) / WIN)
    forward = np.concatenate([np.cos(angle), np.sin(angle)], axis=1) * taper
    weight = np.where(f == 0, 1.0, 2.0) / WIN
    backward = np.concatenate([np.cos(angle) * weight, np.sin(angle) * weight], axis=1) * taper
    return np.stack(two(forward)), np.stack(two(backward.T))


def chip_of(j):
    row, i = divmod(j, 4)
    z, q = divmod(row, 4)
    x = i if row % 2 == 0 else 3 - i
    y = q if z % 2 == 0 else 3 - q
    return x, y, z


def device_of(j, core):
    x, y, z = chip_of(j)
    return (((x // 2 * 4 + y) * 8 + z) * 2 + core) * 2 + x % 2


def permutes(windows):
    partner = [(device_of(j, c), device_of(j, 1 - c)) for j in range(windows) for c in (0, 1)]
    same, cross = [], []
    for j in range(windows - 1):
        same.append((device_of(j + 1, 0), device_of(j, 0)))
        same.append((device_of(j, 1), device_of(j + 1, 1)))
        cross.append((device_of(j + 1, 0), device_of(j, 1)))
        cross.append((device_of(j, 1), device_of(j + 1, 0)))
    return partner, same, cross


def flipped(pairs):
    return [(b, a) for a, b in pairs]


def split(value):
    hi = value.astype(BF16)
    return hi, (value - hi.astype(F32)).astype(BF16)


def stacked(value):
    hi, lo = split(value)
    return jnp.concatenate([hi, lo, hi], axis=0)


def dot(a, b):
    return jnp.dot(a, b, preferred_element_type=F32)


def plane_slot(b):
    j, core = divmod(b, 2)
    row, i = divmod(j, 4)
    x = i if row % 2 == 0 else 3 - i
    return x // 2, row, core, x % 2


def decimate_kernel(taps_ref, raw_ref, out_ref, cur_ref, band_ref, stage_ref, in_sems, out_sems):
    planes = out_ref.shape[2]
    span = TAPS + DEC * BLK
    width = raw_ref.shape[1] // planes
    loads = []
    for plane in range(planes):
        part = pl.ds(plane * width, width)
        loads.append(pltpu.make_async_copy(raw_ref.at[:, part], cur_ref.at[:, part], in_sems.at[plane]))
        loads[-1].start()

    i = lax.broadcasted_iota(jnp.int32, (TAPS, TAPS), 0)
    j = lax.broadcasted_iota(jnp.int32, (TAPS, TAPS), 1)
    mirror = (i + j == TAPS - 1).astype(BF16)
    rows = jnp.broadcast_to(taps_ref[...].astype(F32), (BLK, TAPS))
    mirrored = dot(rows.astype(BF16), mirror)
    wide = jnp.concatenate([mirrored, jnp.zeros((BLK, span - TAPS), F32)], axis=1)
    wide = pltpu.roll(wide, 1, 1, stride=DEC, stride_axis=0)
    band_ref[...] = wide.T.astype(BF16)

    blocks = width // (DEC * BLK)
    group = 16
    band = band_ref[...]
    stores = []
    for plane in range(planes):
        loads[plane].wait()
        for b0 in range(0, blocks, group):
            spans = []
            for b in range(b0, b0 + group):
                start = plane * width + b * DEC * BLK
                if start == 0:
                    tail = jnp.zeros((cur_ref.shape[0], TAPS), BF16)
                    spans.append(jnp.concatenate([tail, cur_ref[:, : DEC * BLK]], axis=1))
                else:
                    spans.append(cur_ref[:, start - TAPS : start + DEC * BLK])
            result = dot(jnp.concatenate(spans, axis=0), band)
            for n in range(group):
                xh, row, core, xl = plane_slot(b0 + n)
                y = row if plane % 2 == 0 else 3 - row
                stage_ref[plane, xh, y, core, xl] = result[n * 16 : (n + 1) * 16]
        stores.append(pltpu.make_async_copy(stage_ref.at[plane], out_ref.at[:, :, plane], out_sems.at[plane]))
        stores[-1].start()
    for store in stores:
        store.wait()


def decimate(raw, taps):
    channels, length = raw.shape
    planes = 8
    return pl.pallas_call(
        decimate_kernel,
        in_specs=[VMEM, ANY],
        out_specs=ANY,
        out_shape=jax.ShapeDtypeStruct((2, 4, planes, 2, 2, channels, BLK), F32),
        scratch_shapes=[
            pltpu.VMEM(raw.shape, BF16),
            pltpu.VMEM((TAPS + DEC * BLK, BLK), BF16),
            pltpu.VMEM((planes, 2, 4, 2, 2, channels, BLK), F32),
            pltpu.SemaphoreType.DMA((planes,)),
            pltpu.SemaphoreType.DMA((planes,)),
        ],
        compiler_params=params(60),
        name="decimate",
    )(taps.reshape(1, TAPS), raw)


def unplane_kernel(in_ref, out_ref):
    planes = in_ref.shape[2]
    for plane in range(planes):
        for b in range(32):
            xh, row, core, xl = plane_slot(b)
            y = row if plane % 2 == 0 else 3 - row
            start = (plane * 32 + b) * BLK
            out_ref[:, start : start + BLK] = in_ref[xh, y, plane, core, xl]


def unplane(blocks):
    planes = blocks.shape[2]
    channels = blocks.shape[5]
    return pl.pallas_call(
        unplane_kernel,
        in_specs=[VMEM],
        out_specs=VMEM,
        out_shape=jax.ShapeDtypeStruct((channels, planes * 32 * BLK), F32),
        compiler_params=params(8),
        name="unplane",
    )(blocks)


def turn(value, k, n):
    re, im = value
    if 8 * abs(k) == n:
        c = np.float32(np.sqrt(0.5))
        return ((re - im) * c, (re + im) * c) if k > 0 else ((re + im) * c, (im - re) * c)
    c, s = np.float32(np.cos(2 * np.pi * k / n)), np.float32(np.sin(2 * np.pi * k / n))
    return re * c - im * s, re * s + im * c


def real_forward(load, n, start, step):
    if n == 2:
        a, b = load(start), load(start + step)
        return [a + b, a - b]
    even = real_forward(load, n // 2, start, 2 * step)
    odd = real_forward(load, n // 2, start + step, 2 * step)
    half, quarter = n // 2, n // 4
    out = [None] * (half + 1)
    out[0], out[half] = even[0] + odd[0], even[0] - odd[0]
    out[quarter] = (even[quarter], -odd[quarter])
    for k in range(1, quarter):
        re, im = turn(odd[k], -k, n)
        er, ei = even[k]
        out[k] = (er + re, ei + im)
        out[half - k] = (er - re, im - ei)
    return out


def real_inverse(bins):
    half = len(bins) - 1
    if half == 1:
        return [bins[0] + bins[1], bins[0] - bins[1]]
    n, quarter = 2 * half, half // 2
    even, odd = [bins[0] + bins[half]], [bins[0] - bins[half]]
    for k in range(1, quarter):
        (ar, ai), (br, bi) = bins[k], bins[half - k]
        even.append((ar + br, ai - bi))
        odd.append(turn((ar - br, ai + bi), k, n))
    re, im = bins[quarter]
    even.append(re + re)
    odd.append(-(im + im))
    out = [None] * n
    out[0::2], out[1::2] = real_inverse(even), real_inverse(odd)
    return out


def real_slot(core, chunk, i):
    s = chunk * WIDTH + i % WIDTH + (HALF if i >= WIDTH else 0)
    return lax.rem(s + HALF * core, SLOTS)


def second_stage(core, chunk, mid_ref, second_ref, own_ref, other_ref):
    for i in range(PART):
        s = real_slot(core, chunk, i)
        wave = dot(second_ref[s], stacked(mid_ref[s]))
        if i < WIDTH:
            own_ref[i] = wave
        else:
            other_ref[i - WIDTH] = wave


def forward_kernel(where_ref, x_ref, second_ref, own_ref, other_ref, mid_ref):
    def tile(t, carry):
        rows = pl.ds(pl.multiple_of(t * 8, 8), 8)
        rows_im = pl.ds(pl.multiple_of(ROOT + t * 8, 8), 8)
        bins = real_forward(lambda c1: x_ref[c1, rows, :], ROOT, 0, 1)
        mid_ref[0, rows, :] = bins[0]
        mid_ref[0, rows_im, :] = bins[SLOTS]
        for s in range(1, SLOTS):
            mid_ref[s, rows, :], mid_ref[s, rows_im, :] = bins[s]
        return carry

    lax.fori_loop(0, ROOT // 8, tile, 0)
    second_stage(where_ref[0], 0, mid_ref, second_ref, own_ref, other_ref)


def forward_space(where, x, second):
    return pl.pallas_call(
        forward_kernel,
        in_specs=[SMEM] + [VMEM] * 2,
        out_specs=[VMEM] * 3,
        out_shape=[WAVE, WAVE, jax.ShapeDtypeStruct((SLOTS, BLK, BLK), F32)],
        compiler_params=params(14),
        name="forward_space",
    )(where, x.reshape(ROOT, ROOT, BLK), second)


def forward_more_kernel(chunk, where_ref, mid_ref, second_ref, own_ref, other_ref):
    second_stage(where_ref[0], chunk, mid_ref, second_ref, own_ref, other_ref)


def forward_more(chunk, where, middle, second):
    return pl.pallas_call(
        functools.partial(forward_more_kernel, chunk),
        in_specs=[SMEM] + [VMEM] * 2,
        out_specs=[VMEM] * 2,
        out_shape=[WAVE, WAVE],
        compiler_params=params(12),
        name="forward_more",
    )(where, middle, second)


def inverse_stage(core, chunk, own_ref, halo_ref, part_ref, cross_ref, inv_ref, mid_ref):
    for i in range(PART):
        if i < WIDTH:
            z = own_ref[i] + halo_ref[i]
        else:
            z = part_ref[i - WIDTH] + cross_ref[i - WIDTH]
        mid_ref[i] = dot(inv_ref[real_slot(core, chunk, i)], stacked(z))


def inverse_more_kernel(chunk, where_ref, own_ref, halo_ref, part_ref, cross_ref, inv_ref, mid_ref):
    inverse_stage(where_ref[0], chunk, own_ref, halo_ref, part_ref, cross_ref, inv_ref, mid_ref)


def inverse_more(chunk, where, waves, inv):
    return pl.pallas_call(
        functools.partial(inverse_more_kernel, chunk),
        in_specs=[SMEM] + [VMEM] * 5,
        out_specs=VMEM,
        out_shape=MIDDLE,
        compiler_params=params(12),
        name="inverse_more",
    )(where, *waves, inv)


def inverse_kernel(where_ref, own_ref, halo_ref, part_ref, cross_ref, inv_ref, *rest):
    earlier, out_ref, mid_ref = rest[:-2], rest[-2], rest[-1]
    core = where_ref[0]
    inverse_stage(core, CHUNKS - 1, own_ref, halo_ref, part_ref, cross_ref, inv_ref, mid_ref)
    refs = earlier + (mid_ref,)

    def tile(t, carry):
        rows = pl.ds(pl.multiple_of(t * 8, 8), 8)
        rows_im = pl.ds(pl.multiple_of(ROOT + t * 8, 8), 8)

        def both(s):
            ref = refs[s % HALF // WIDTH]
            place = s % WIDTH + WIDTH * lax.rem(core + s // HALF, 2)
            return ref[place, rows, :], ref[place, rows_im, :]

        low, high = both(0)
        values = real_inverse([low] + [both(s) for s in range(1, SLOTS)] + [high])
        for c1 in range(ROOT):
            out_ref[c1, rows, :] = values[c1]
        return carry

    lax.fori_loop(0, ROOT // 8, tile, 0)


def inverse_space(where, waves, earlier, inv):
    return pl.pallas_call(
        inverse_kernel,
        in_specs=[SMEM] + [VMEM] * (5 + len(earlier)),
        out_specs=VMEM,
        out_shape=jax.ShapeDtypeStruct((ROOT, ROOT, BLK), F32),
        scratch_shapes=[pltpu.VMEM(MIDDLE.shape, F32)],
        compiler_params=params(14),
        name="inverse_space",
    )(where, *waves, inv, *earlier)


def gains_kernel(where_ref, gain_ref, band_ref, out_ref):
    core = where_ref[0]
    n = ROOT // 2
    i = lax.broadcasted_iota(jnp.int32, (ROOT, ROOT), 0)
    j = lax.broadcasted_iota(jnp.int32, (ROOT, ROOT), 1)
    mirror = (i + j == ROOT - 1).astype(BF16)
    source = jnp.where(i == 0, 0, jnp.where(i < n, n - i, n + ROOT - 1 - i))
    mirror0 = (j == source).astype(BF16)

    def rows(k1, k2, count):
        return band_ref[pl.ds(k1 + ROOT * k2, count, stride=ROOT), :]

    def exact(perm, bands):
        return dot(perm, bands.astype(F32).astype(BF16))

    def pick(bands):
        total = jnp.zeros(bands.shape, F32)
        for b in range(BANDS):
            total = jnp.where(bands == b, gain_ref[b], total)
        return total

    def put(s, plus, minus):
        gp, gm = pick(plus.astype(F32)), pick(minus)
        out_ref[0, s] = gp + gm
        out_ref[1, s] = gp - gm

    for s in range(HALF):
        if s:
            k1 = s + HALF * core
            put(s, rows(k1, 0, ROOT), exact(mirror, rows(ROOT - k1, 0, ROOT)))
            continue

        @pl.when(core == 0)
        def _():
            plus = jnp.concatenate([rows(0, 0, n), rows(n, 0, n)], axis=0)
            minus = jnp.concatenate([rows(0, n, n), rows(n, n, n)], axis=0)
            put(0, plus, exact(mirror0, minus))

        @pl.when(core != 0)
        def _():
            put(0, rows(HALF, 0, ROOT), exact(mirror, rows(ROOT - HALF, 0, ROOT)))


def gains(where, band_gain, fan_band):
    return pl.pallas_call(
        gains_kernel,
        in_specs=[SMEM] * 2 + [VMEM],
        out_specs=VMEM,
        out_shape=jax.ShapeDtypeStruct((2, HALF, ROOT, BLK), F32),
        compiler_params=params(8),
        name="gains",
    )(where, band_gain, fan_band)


def time_kernel(first_chunk, where_ref, *refs):
    own_ref, part_ref, same_ref, cross_ref, mine_ref, theirs_ref, fwd_ref, bwd_ref = refs[:8]
    out_refs = refs[8:]
    core, xl = where_ref[0], where_ref[1]
    step = pl.program_id(0)
    slots = own_ref.shape[0]
    rows = slots * BLK
    even = core == 0

    def flat(ref):
        return ref[...].reshape(rows, BLK)

    own, part, same, cross = flat(own_ref), flat(part_ref), flat(same_ref), flat(cross_ref)
    x = jnp.concatenate(
        [
            jnp.where(even, cross, same),
            jnp.where(even, own, part),
            jnp.where(even, part, own),
            jnp.where(even, same, cross),
        ],
        axis=1,
    )
    hi, lo = split(x)
    fwd_hi = fwd_ref[0]
    v = dot(hi, fwd_hi) + dot(lo, fwd_hi) + dot(hi, fwd_ref[1])
    pieces = []
    for s in range(slots):
        p = v[s * BLK : s * BLK + ROOT]
        q = v[s * BLK + ROOT : (s + 1) * BLK]
        a, d = p[:, :BINS], p[:, BINS:]
        c, b = q[:, :BINS], q[:, BINS:]

        def wide(kind):
            mine, theirs = mine_ref[kind, s], theirs_ref[kind, s]
            low = jnp.where(xl == 0, mine, theirs)
            high = jnp.where(xl == 0, theirs, mine)
            return jnp.concatenate([low, high], axis=1)

        gs, gd = wide(0), wide(1)
        gr = gi = gs
        if s == 0 and first_chunk:
            row = lax.broadcasted_iota(jnp.int32, (ROOT, BINS), 0)
            pair = (row == 0) & (step == 0) & even
            gr = jnp.where(pair, gs + gd, gs)
            gi = jnp.where(pair, gs - gd, gs)
            gd = jnp.where(pair, 0.0, gd)
        pieces.append(jnp.concatenate([gr * a + gd * b, gr * d - gd * c], axis=1))
        pieces.append(jnp.concatenate([gi * c - gd * d, gd * a + gi * b], axis=1))
    hi, lo = split(jnp.concatenate(pieces, axis=0))
    bwd_hi = bwd_ref[0]
    z = dot(hi, bwd_hi) + dot(lo, bwd_hi) + dot(hi, bwd_ref[1])
    before, low, high, after = (z[:, n * BLK : (n + 1) * BLK] for n in range(4))
    outs = [
        jnp.where(even, low, high),
        jnp.where(even, high, low),
        jnp.where(even, after, before),
        jnp.where(even, before, after),
    ]
    for out_ref, value in zip(out_refs, outs):
        out_ref[...] = value.reshape(slots, BLK, BLK)


def time_filter(chunk, where, waves, mine, theirs, fwd, bwd):
    slots = 4
    steps = WIDTH // slots
    data = pl.BlockSpec((slots, BLK, BLK), lambda g: (g, 0, 0))
    gain = pl.BlockSpec((2, slots, ROOT, BLK), lambda g: (0, chunk * steps + g, 0, 0))
    table = pl.BlockSpec((2, WIN, WIN), lambda g: (0, 0, 0))
    return pl.pallas_call(
        functools.partial(time_kernel, chunk == 0),
        grid=(steps,),
        in_specs=[SMEM] + [data] * 4 + [gain] * 2 + [table] * 2,
        out_specs=[data] * 4,
        out_shape=[jax.ShapeDtypeStruct((WIDTH, BLK, BLK), F32)] * 4,
        compiler_params=params(24),
        name="time_filter",
    )(where, *waves, mine, theirs, fwd, bwd)


def body(raw_strain, fir_taps, fan_band, band_gain):
    where = jnp.stack([lax.axis_index("chan") % 2, lax.axis_index("tile")]).astype(jnp.int32)
    second, inverse = (jnp.asarray(t) for t in spatial_tables())
    fwd, bwd = (jnp.asarray(t) for t in temporal_tables())
    partner, same, cross = permutes(raw_strain.shape[1] // DEC // HOP)

    mine = gains(where, band_gain, fan_band)
    theirs = lax.ppermute(mine, "tile", [(0, 1), (1, 0)])

    blocks = decimate(raw_strain, fir_taps)
    shape = blocks.shape
    blocks = blocks.reshape((256,) + shape[5:])
    blocks = lax.all_to_all(blocks, AXES, 0, 0, tiled=True)
    own, other, middle = forward_space(where, blocks, second)
    received = []
    for g in range(CHUNKS):
        if g:
            own, other = forward_more(g, where, middle, second)
        from_partner = lax.ppermute(other, AXES, partner)
        from_same = lax.ppermute(own, AXES, same)
        from_cross = lax.ppermute(other, AXES, cross)
        received.append((own, from_partner, from_same, from_cross))
    returned = []
    for g in range(CHUNKS):
        own, part, halo, far = time_filter(g, where, received[g], mine, theirs, fwd, bwd)
        back_partner = lax.ppermute(part, AXES, partner)
        back_same = lax.ppermute(halo, AXES, flipped(same))
        back_cross = lax.ppermute(far, AXES, flipped(cross))
        returned.append((own, back_same, back_partner, back_cross))
    earlier = [inverse_more(g, where, returned[g], inverse) for g in range(CHUNKS - 1)]
    filtered = inverse_space(where, returned[-1], earlier, inverse)
    filtered = lax.all_to_all(filtered.reshape(256, 16, BLK), AXES, 0, 0, tiled=True)
    return unplane(filtered.reshape(shape))


def solution(mesh):
    return jax.shard_map(
        body,
        mesh=mesh,
        in_specs=(P(AXES, None), P(), P(None, "tile"), P()),
        out_specs=P(AXES, None),
        check_vma=False,
    )
```

```python
import functools

import jax
import jax.numpy as jnp
import numpy as np
from jax import lax
from jax.experimental import pallas as pl
from jax.experimental.pallas import tpu as pltpu
from jax.sharding import PartitionSpec as P
import ml_dtypes

K = 4096
ROOT = 64
WIN = 512
TAPS = 128
DEC = 4
BANDS = 8
HOP = 256
BINS = 256
BLK = 128
SLOTS = 32
HALF = 16
CHUNKS = 2
WIDTH = HALF // CHUNKS
PART = 2 * WIDTH
AXES = ("chan", "tile")
F32 = jnp.float32
BF16 = jnp.bfloat16
MIB = 1024 * 1024
WAVE = jax.ShapeDtypeStruct((WIDTH, BLK, BLK), F32)
MIDDLE = jax.ShapeDtypeStruct((PART, BLK, BLK), F32)


def params(mib):
    return pltpu.CompilerParams(vmem_limit_bytes=mib * MIB)


VMEM = pl.BlockSpec(memory_space=pltpu.VMEM)
SMEM = pl.BlockSpec(memory_space=pltpu.SMEM)
ANY = pl.BlockSpec(memory_space=pl.ANY)


def two(table):
    table = np.asarray(table, np.float32)
    hi = table.astype(ml_dtypes.bfloat16)
    lo = (table - hi.astype(np.float32)).astype(ml_dtypes.bfloat16)
    return hi, lo


def left_operand(table):
    hi, lo = two(table)
    return np.concatenate([hi, hi, lo], axis=-1)


def spatial_tables():
    c0 = np.arange(ROOT)[None, :]
    k2 = np.arange(ROOT)[:, None]
    second = np.zeros((SLOTS, 2, ROOT, 2, ROOT))
    inverse = np.zeros((SLOTS, 2, ROOT, 2, ROOT))
    for s in range(SLOTS):
        phase = 2 * np.pi / K * ((s + ROOT * k2) * c0 % K)
        co, si = np.cos(phase), np.sin(phase)
        if s:
            second[s, 0, :, 0], second[s, 0, :, 1] = co, si
            second[s, 1, :, 0], second[s, 1, :, 1] = -si, co
            inverse[s, 0, :, 0], inverse[s, 0, :, 1] = co.T / 2, -si.T / 2
            inverse[s, 1, :, 0], inverse[s, 1, :, 1] = si.T / 2, co.T / 2
            continue
        n = ROOT // 2
        second[0, 0, :n, 0], second[0, 1, :n, 0] = co[:n], -si[:n]
        second[0, 1, 0, 0] = (-1.0) ** c0[0]
        inverse[0, 0, :, 0, :n], inverse[0, 0, :, 1, :n] = co[:n].T, -si[:n].T
        inverse[0, 0, :, 0, 0] = 0.5
        inverse[0, 0, :, 1, 0] = 0.5 * (-1.0) ** c0[0]
        phase = 2 * np.pi / K * ((n + ROOT * k2[:n]) * c0 % K)
        co, si = np.cos(phase), np.sin(phase)
        second[0, 0, n:, 1], second[0, 1, n:, 1] = co, -si
        inverse[0, 1, :, 0, n:], inverse[0, 1, :, 1, n:] = co.T, -si.T
    second = second.reshape(SLOTS, BLK, BLK)
    inverse = inverse.reshape(SLOTS, BLK, BLK) / K
    return left_operand(second), left_operand(inverse)


def temporal_tables():
    s = np.arange(WIN)[:, None]
    f = np.arange(BINS)[None, :]
    angle = 2 * np.pi / WIN * (s * f % WIN)
    taper = np.sin(np.pi * (s + 0.5) / WIN)
    forward = np.concatenate([np.cos(angle), np.sin(angle)], axis=1) * taper
    weight = np.where(f == 0, 1.0, 2.0) / WIN
    backward = np.concatenate([np.cos(angle) * weight, np.sin(angle) * weight], axis=1) * taper
    return np.stack(two(forward)), np.stack(two(backward.T))


def chip_of(j):
    row, i = divmod(j, 4)
    z, q = divmod(row, 4)
    x = i if row % 2 == 0 else 3 - i
    y = q if z % 2 == 0 else 3 - q
    return x, y, z


def device_of(j, core):
    x, y, z = chip_of(j)
    return (((x // 2 * 4 + y) * 8 + z) * 2 + core) * 2 + x % 2


def permutes(windows):
    partner = [(device_of(j, c), device_of(j, 1 - c)) for j in range(windows) for c in (0, 1)]
    same, cross = [], []
    for j in range(windows - 1):
        same.append((device_of(j + 1, 0), device_of(j, 0)))
        same.append((device_of(j, 1), device_of(j + 1, 1)))
        cross.append((device_of(j + 1, 0), device_of(j, 1)))
        cross.append((device_of(j, 1), device_of(j + 1, 0)))
    return partner, same, cross


def flipped(pairs):
    return [(b, a) for a, b in pairs]


def core_index():
    return lax.rem(lax.axis_index("chan"), 2)


def split(value):
    hi = value.astype(BF16)
    return hi, (value - hi.astype(F32)).astype(BF16)


def stacked(value):
    hi, lo = split(value)
    return jnp.concatenate([hi, lo, hi], axis=0)


def dot(a, b):
    return jnp.dot(a, b, preferred_element_type=F32)


def plane_slot(b):
    j, core = divmod(b, 2)
    row, i = divmod(j, 4)
    x = i if row % 2 == 0 else 3 - i
    return x // 2, row, core, x % 2


def decimate_kernel(taps_hbm, raw_ref, out_ref, taps_ref, cur_ref, band_ref, stage_ref, in_sems, out_sems):
    planes = out_ref.shape[2]
    span = TAPS + DEC * BLK
    width = raw_ref.shape[1] // planes
    pair = 2
    loads = []
    for n in range(planes // pair):
        part = pl.ds(n * pair * width, pair * width)
        loads.append(pltpu.make_async_copy(raw_ref.at[:, part], cur_ref.at[:, part], in_sems.at[n]))
        loads[-1].start()
        if n == 0:
            taps_load = pltpu.make_async_copy(taps_hbm, taps_ref, in_sems.at[planes])
            taps_load.start()
    taps_load.wait()

    i = lax.broadcasted_iota(jnp.int32, (TAPS, TAPS), 0)
    j = lax.broadcasted_iota(jnp.int32, (TAPS, TAPS), 1)
    mirror = (i + j == TAPS - 1).astype(BF16)
    rows = jnp.broadcast_to(taps_ref[...].astype(F32), (BLK, TAPS))
    mirrored = dot(rows.astype(BF16), mirror)
    wide = jnp.concatenate([mirrored, jnp.zeros((BLK, span - TAPS), F32)], axis=1)
    wide = pltpu.roll(wide, 1, 1, stride=DEC, stride_axis=0)
    band_ref[...] = wide.T.astype(BF16)

    blocks = width // (DEC * BLK)
    group = 16
    band = band_ref[...]
    stores = []
    for plane in range(planes):
        if plane % pair == 0:
            loads[plane // pair].wait()
        for b0 in range(0, blocks, group):
            spans = []
            for b in range(b0, b0 + group):
                start = plane * width + b * DEC * BLK
                if start == 0:
                    tail = jnp.zeros((cur_ref.shape[0], TAPS), BF16)
                    spans.append(jnp.concatenate([tail, cur_ref[:, : DEC * BLK]], axis=1))
                else:
                    spans.append(cur_ref[:, start - TAPS : start + DEC * BLK])
            result = dot(jnp.concatenate(spans, axis=0), band)
            for n in range(group):
                xh, row, core, xl = plane_slot(b0 + n)
                y = row if plane % 2 == 0 else 3 - row
                stage_ref[plane, xh, y, core, xl] = result[n * 16 : (n + 1) * 16]
        stores.append(pltpu.make_async_copy(stage_ref.at[plane], out_ref.at[:, :, plane], out_sems.at[plane]))
        stores[-1].start()
    for store in stores:
        store.wait()


def decimate(raw, taps):
    channels, length = raw.shape
    planes = 8
    return pl.pallas_call(
        decimate_kernel,
        in_specs=[ANY, ANY],
        out_specs=ANY,
        out_shape=jax.ShapeDtypeStruct((2, 4, planes, 2, 2, channels, BLK), F32),
        scratch_shapes=[
            pltpu.VMEM((1, TAPS), BF16),
            pltpu.VMEM(raw.shape, BF16),
            pltpu.VMEM((TAPS + DEC * BLK, BLK), BF16),
            pltpu.VMEM((planes, 2, 4, 2, 2, channels, BLK), F32),
            pltpu.SemaphoreType.DMA((planes + 1,)),
            pltpu.SemaphoreType.DMA((planes,)),
        ],
        compiler_params=params(60),
        name="decimate",
    )(taps.reshape(1, TAPS), raw)


def unplane_kernel(in_ref, out_ref):
    planes = in_ref.shape[2]
    for plane in range(planes):
        for b in range(32):
            xh, row, core, xl = plane_slot(b)
            y = row if plane % 2 == 0 else 3 - row
            start = (plane * 32 + b) * BLK
            out_ref[:, start : start + BLK] = in_ref[xh, y, plane, core, xl]


def unplane(blocks):
    planes = blocks.shape[2]
    channels = blocks.shape[5]
    return pl.pallas_call(
        unplane_kernel,
        in_specs=[VMEM],
        out_specs=VMEM,
        out_shape=jax.ShapeDtypeStruct((channels, planes * 32 * BLK), F32),
        compiler_params=params(8),
        name="unplane",
    )(blocks)


def turn(value, k, n):
    re, im = value
    if 8 * abs(k) == n:
        c = np.float32(np.sqrt(0.5))
        return ((re - im) * c, (re + im) * c) if k > 0 else ((re + im) * c, (im - re) * c)
    c, s = np.float32(np.cos(2 * np.pi * k / n)), np.float32(np.sin(2 * np.pi * k / n))
    return re * c - im * s, re * s + im * c


def real_forward(load, n, start, step):
    if n == 2:
        a, b = load(start), load(start + step)
        return [a + b, a - b]
    even = real_forward(load, n // 2, start, 2 * step)
    odd = real_forward(load, n // 2, start + step, 2 * step)
    half, quarter = n // 2, n // 4
    out = [None] * (half + 1)
    out[0], out[half] = even[0] + odd[0], even[0] - odd[0]
    out[quarter] = (even[quarter], -odd[quarter])
    for k in range(1, quarter):
        re, im = turn(odd[k], -k, n)
        er, ei = even[k]
        out[k] = (er + re, ei + im)
        out[half - k] = (er - re, im - ei)
    return out


def real_inverse(bins):
    half = len(bins) - 1
    if half == 1:
        return [bins[0] + bins[1], bins[0] - bins[1]]
    n, quarter = 2 * half, half // 2
    even, odd = [bins[0] + bins[half]], [bins[0] - bins[half]]
    for k in range(1, quarter):
        (ar, ai), (br, bi) = bins[k], bins[half - k]
        even.append((ar + br, ai - bi))
        odd.append(turn((ar - br, ai + bi), k, n))
    re, im = bins[quarter]
    even.append(re + re)
    odd.append(-(im + im))
    out = [None] * n
    out[0::2], out[1::2] = real_inverse(even), real_inverse(odd)
    return out


def real_slot(core, chunk, i):
    s = chunk * WIDTH + i % WIDTH + (HALF if i >= WIDTH else 0)
    return lax.rem(s + HALF * core, SLOTS)


def second_stage(core, chunk, mid_ref, second_ref, own_ref, other_ref):
    for i in range(PART):
        s = real_slot(core, chunk, i)
        wave = dot(second_ref[s], stacked(mid_ref[s]))
        if i < WIDTH:
            own_ref[i] = wave
        else:
            other_ref[i - WIDTH] = wave


def forward_kernel(x_hbm, second_ref, own_ref, other_ref, mid_ref, x_ref, sems):
    half = ROOT // 2
    loads = []
    for n in range(2):
        part = pl.ds(n * half, half)
        loads.append(pltpu.make_async_copy(x_hbm.at[:, part], x_ref.at[:, part], sems.at[n]))
        loads[-1].start()

    def tile(t, carry):
        rows = pl.ds(pl.multiple_of(t * 8, 8), 8)
        rows_im = pl.ds(pl.multiple_of(ROOT + t * 8, 8), 8)
        bins = real_forward(lambda c1: x_ref[c1, rows, :], ROOT, 0, 1)
        mid_ref[0, rows, :] = bins[0]
        mid_ref[0, rows_im, :] = bins[SLOTS]
        for s in range(1, SLOTS):
            mid_ref[s, rows, :], mid_ref[s, rows_im, :] = bins[s]
        return carry

    for n in range(2):
        loads[n].wait()
        lax.fori_loop(n * half // 8, (n + 1) * half // 8, tile, 0)
    second_stage(core_index(), 0, mid_ref, second_ref, own_ref, other_ref)


def forward_space(x, second):
    return pl.pallas_call(
        forward_kernel,
        in_specs=[ANY, VMEM],
        out_specs=[VMEM] * 3,
        out_shape=[WAVE, WAVE, jax.ShapeDtypeStruct((SLOTS, BLK, BLK), F32)],
        scratch_shapes=[pltpu.VMEM((ROOT, ROOT, BLK), F32), pltpu.SemaphoreType.DMA((2,))],
        compiler_params=params(14),
        name="forward_space",
    )(x.reshape(ROOT, ROOT, BLK), second)


def forward_more_kernel(chunk, mid_ref, second_ref, own_ref, other_ref):
    second_stage(core_index(), chunk, mid_ref, second_ref, own_ref, other_ref)


def forward_more(chunk, middle, second):
    return pl.pallas_call(
        functools.partial(forward_more_kernel, chunk),
        in_specs=[VMEM] * 2,
        out_specs=[VMEM] * 2,
        out_shape=[WAVE, WAVE],
        compiler_params=params(12),
        name="forward_more",
    )(middle, second)


def inverse_stage(core, chunk, own_ref, halo_ref, part_ref, cross_ref, inv_ref, mid_ref):
    for i in range(PART):
        if i < WIDTH:
            z = own_ref[i] + halo_ref[i]
        else:
            z = part_ref[i - WIDTH] + cross_ref[i - WIDTH]
        mid_ref[i] = dot(inv_ref[real_slot(core, chunk, i)], stacked(z))


def inverse_more_kernel(chunk, own_ref, halo_ref, part_ref, cross_ref, inv_ref, mid_ref):
    inverse_stage(core_index(), chunk, own_ref, halo_ref, part_ref, cross_ref, inv_ref, mid_ref)


def inverse_more(chunk, waves, inv):
    return pl.pallas_call(
        functools.partial(inverse_more_kernel, chunk),
        in_specs=[VMEM] * 5,
        out_specs=VMEM,
        out_shape=MIDDLE,
        compiler_params=params(12),
        name="inverse_more",
    )(*waves, inv)


def inverse_kernel(own_ref, halo_ref, part_ref, cross_ref, inv_ref, *rest):
    earlier, out_ref, mid_ref = rest[:-2], rest[-2], rest[-1]
    core = core_index()
    inverse_stage(core, CHUNKS - 1, own_ref, halo_ref, part_ref, cross_ref, inv_ref, mid_ref)
    refs = earlier + (mid_ref,)

    def tile(t, carry):
        rows = pl.ds(pl.multiple_of(t * 8, 8), 8)
        rows_im = pl.ds(pl.multiple_of(ROOT + t * 8, 8), 8)

        def both(s):
            ref = refs[s % HALF // WIDTH]
            place = s % WIDTH + WIDTH * lax.rem(core + s // HALF, 2)
            return ref[place, rows, :], ref[place, rows_im, :]

        low, high = both(0)
        values = real_inverse([low] + [both(s) for s in range(1, SLOTS)] + [high])
        for c1 in range(ROOT):
            out_ref[c1, rows, :] = values[c1]
        return carry

    lax.fori_loop(0, ROOT // 8, tile, 0)


def inverse_space(waves, earlier, inv):
    return pl.pallas_call(
        inverse_kernel,
        in_specs=[VMEM] * (5 + len(earlier)),
        out_specs=VMEM,
        out_shape=jax.ShapeDtypeStruct((ROOT, ROOT, BLK), F32),
        scratch_shapes=[pltpu.VMEM(MIDDLE.shape, F32)],
        compiler_params=params(14),
        name="inverse_space",
    )(*waves, inv, *earlier)


def gains_kernel(gain_ref, band_ref, out_ref):
    core = core_index()
    n = ROOT // 2
    i = lax.broadcasted_iota(jnp.int32, (ROOT, ROOT), 0)
    j = lax.broadcasted_iota(jnp.int32, (ROOT, ROOT), 1)
    mirror = (i + j == ROOT - 1).astype(BF16)
    source = jnp.where(i == 0, 0, jnp.where(i < n, n - i, n + ROOT - 1 - i))
    mirror0 = (j == source).astype(BF16)

    def rows(k1, k2, count):
        return band_ref[pl.ds(k1 + ROOT * k2, count, stride=ROOT), :]

    def exact(perm, bands):
        return dot(perm, bands.astype(F32).astype(BF16))

    def pick(bands):
        total = jnp.zeros(bands.shape, F32)
        for b in range(BANDS):
            total = jnp.where(bands == b, gain_ref[b], total)
        return total

    def put(s, plus, minus):
        gp, gm = pick(plus.astype(F32)), pick(minus)
        out_ref[0, s] = gp + gm
        out_ref[1, s] = gp - gm

    for s in range(HALF):
        if s:
            k1 = s + HALF * core
            put(s, rows(k1, 0, ROOT), exact(mirror, rows(ROOT - k1, 0, ROOT)))
            continue

        @pl.when(core == 0)
        def _():
            plus = jnp.concatenate([rows(0, 0, n), rows(n, 0, n)], axis=0)
            minus = jnp.concatenate([rows(0, n, n), rows(n, n, n)], axis=0)
            put(0, plus, exact(mirror0, minus))

        @pl.when(core != 0)
        def _():
            put(0, rows(HALF, 0, ROOT), exact(mirror, rows(ROOT - HALF, 0, ROOT)))


def gains(band_gain, fan_band):
    return pl.pallas_call(
        gains_kernel,
        in_specs=[SMEM, VMEM],
        out_specs=VMEM,
        out_shape=jax.ShapeDtypeStruct((2, HALF, ROOT, BLK), F32),
        compiler_params=params(8),
        name="gains",
    )(band_gain, fan_band)


def time_kernel(first_chunk, *refs):
    own_ref, part_ref, same_ref, cross_ref, mine_ref, theirs_ref, fwd_ref, bwd_ref = refs[:8]
    out_refs = refs[8:]
    core, xl = core_index(), lax.axis_index("tile")
    step = pl.program_id(0)
    slots = own_ref.shape[0]
    rows = slots * BLK
    even = core == 0

    def flat(ref):
        return ref[...].reshape(rows, BLK)

    own, part, same, cross = flat(own_ref), flat(part_ref), flat(same_ref), flat(cross_ref)
    x = jnp.concatenate(
        [
            jnp.where(even, cross, same),
            jnp.where(even, own, part),
            jnp.where(even, part, own),
            jnp.where(even, same, cross),
        ],
        axis=1,
    )
    hi, lo = split(x)
    fwd_hi = fwd_ref[0]
    v = dot(hi, fwd_hi) + dot(lo, fwd_hi) + dot(hi, fwd_ref[1])
    pieces = []
    for s in range(slots):
        p = v[s * BLK : s * BLK + ROOT]
        q = v[s * BLK + ROOT : (s + 1) * BLK]
        a, d = p[:, :BINS], p[:, BINS:]
        c, b = q[:, :BINS], q[:, BINS:]

        def wide(kind):
            mine, theirs = mine_ref[kind, s], theirs_ref[kind, s]
            low = jnp.where(xl == 0, mine, theirs)
            high = jnp.where(xl == 0, theirs, mine)
            return jnp.concatenate([low, high], axis=1)

        gs, gd = wide(0), wide(1)
        gr = gi = gs
        if s == 0 and first_chunk:
            row = lax.broadcasted_iota(jnp.int32, (ROOT, BINS), 0)
            pair = (row == 0) & (step == 0) & even
            gr = jnp.where(pair, gs + gd, gs)
            gi = jnp.where(pair, gs - gd, gs)
            gd = jnp.where(pair, 0.0, gd)
        pieces.append(jnp.concatenate([gr * a + gd * b, gr * d - gd * c], axis=1))
        pieces.append(jnp.concatenate([gi * c - gd * d, gd * a + gi * b], axis=1))
    hi, lo = split(jnp.concatenate(pieces, axis=0))
    bwd_hi = bwd_ref[0]
    z = dot(hi, bwd_hi) + dot(lo, bwd_hi) + dot(hi, bwd_ref[1])
    before, low, high, after = (z[:, n * BLK : (n + 1) * BLK] for n in range(4))
    outs = [
        jnp.where(even, low, high),
        jnp.where(even, high, low),
        jnp.where(even, after, before),
        jnp.where(even, before, after),
    ]
    for out_ref, value in zip(out_refs, outs):
        out_ref[...] = value.reshape(slots, BLK, BLK)


def time_filter(chunk, waves, mine, theirs, fwd, bwd):
    slots = 4
    steps = WIDTH // slots
    data = pl.BlockSpec((slots, BLK, BLK), lambda g: (g, 0, 0))
    gain = pl.BlockSpec((2, slots, ROOT, BLK), lambda g: (0, chunk * steps + g, 0, 0))
    table = pl.BlockSpec((2, WIN, WIN), lambda g: (0, 0, 0))
    return pl.pallas_call(
        functools.partial(time_kernel, chunk == 0),
        grid=(steps,),
        in_specs=[data] * 4 + [gain] * 2 + [table] * 2,
        out_specs=[data] * 4,
        out_shape=[jax.ShapeDtypeStruct((WIDTH, BLK, BLK), F32)] * 4,
        compiler_params=params(24),
        name="time_filter",
    )(*waves, mine, theirs, fwd, bwd)


def body(raw_strain, fir_taps, fan_band, band_gain):
    second, inverse = (jnp.asarray(t) for t in spatial_tables())
    fwd, bwd = (jnp.asarray(t) for t in temporal_tables())
    partner, same, cross = permutes(raw_strain.shape[1] // DEC // HOP)

    mine = gains(band_gain, fan_band)
    theirs = lax.ppermute(mine, "tile", [(0, 1), (1, 0)])

    blocks = decimate(raw_strain, fir_taps)
    shape = blocks.shape
    blocks = blocks.reshape((256,) + shape[5:])
    blocks = lax.all_to_all(blocks, AXES, 0, 0, tiled=True)
    own, other, middle = forward_space(blocks, second)
    received = []
    for g in range(CHUNKS):
        if g:
            own, other = forward_more(g, middle, second)
        from_partner = lax.ppermute(other, AXES, partner)
        from_same = lax.ppermute(own, AXES, same)
        from_cross = lax.ppermute(other, AXES, cross)
        received.append((own, from_partner, from_same, from_cross))
    returned = []
    for g in range(CHUNKS):
        own, part, halo, far = time_filter(g, received[g], mine, theirs, fwd, bwd)
        back_partner = lax.ppermute(part, AXES, partner)
        back_same = lax.ppermute(halo, AXES, flipped(same))
        back_cross = lax.ppermute(far, AXES, flipped(cross))
        returned.append((own, back_same, back_partner, back_cross))
    earlier = [inverse_more(g, returned[g], inverse) for g in range(CHUNKS - 1)]
    filtered = inverse_space(returned[-1], earlier, inverse)
    filtered = lax.all_to_all(filtered.reshape(256, 16, BLK), AXES, 0, 0, tiled=True)
    return unplane(filtered.reshape(shape))


def solution(mesh):
    return jax.shard_map(
        body,
        mesh=mesh,
        in_specs=(P(AXES, None), P(), P(None, "tile"), P()),
        out_specs=P(AXES, None),
        check_vma=False,
    )
```

```python
import functools

import jax
import jax.numpy as jnp
import numpy as np
from jax import lax
from jax.experimental import pallas as pl
from jax.experimental.pallas import tpu as pltpu
from jax.sharding import PartitionSpec as P
import ml_dtypes

K = 4096
ROOT = 64
WIN = 512
TAPS = 128
DEC = 4
BANDS = 8
HOP = 256
BINS = 256
BLK = 128
SLOTS = 32
HALF = 16
CHUNKS = 2
WIDTH = HALF // CHUNKS
PART = 2 * WIDTH
AXES = ("chan", "tile")
F32 = jnp.float32
BF16 = jnp.bfloat16
MIB = 1024 * 1024
WAVE = jax.ShapeDtypeStruct((WIDTH, BLK, BLK), F32)
MIDDLE = jax.ShapeDtypeStruct((PART, BLK, BLK), F32)


def params(mib):
    return pltpu.CompilerParams(vmem_limit_bytes=mib * MIB)


VMEM = pl.BlockSpec(memory_space=pltpu.VMEM)
SMEM = pl.BlockSpec(memory_space=pltpu.SMEM)
ANY = pl.BlockSpec(memory_space=pl.ANY)


def two(table):
    table = np.asarray(table, np.float32)
    hi = table.astype(ml_dtypes.bfloat16)
    lo = (table - hi.astype(np.float32)).astype(ml_dtypes.bfloat16)
    return hi, lo


def left_operand(table):
    hi, lo = two(table)
    return np.concatenate([hi, hi, lo], axis=-1)


def spatial_tables():
    c0 = np.arange(ROOT)[None, :]
    k2 = np.arange(ROOT)[:, None]
    second = np.zeros((SLOTS, 2, ROOT, 2, ROOT))
    inverse = np.zeros((SLOTS, 2, ROOT, 2, ROOT))
    for s in range(SLOTS):
        phase = 2 * np.pi / K * ((s + ROOT * k2) * c0 % K)
        co, si = np.cos(phase), np.sin(phase)
        if s:
            second[s, 0, :, 0], second[s, 0, :, 1] = co, si
            second[s, 1, :, 0], second[s, 1, :, 1] = -si, co
            inverse[s, 0, :, 0], inverse[s, 0, :, 1] = co.T / 2, -si.T / 2
            inverse[s, 1, :, 0], inverse[s, 1, :, 1] = si.T / 2, co.T / 2
            continue
        n = ROOT // 2
        second[0, 0, :n, 0], second[0, 1, :n, 0] = co[:n], -si[:n]
        second[0, 1, 0, 0] = (-1.0) ** c0[0]
        inverse[0, 0, :, 0, :n], inverse[0, 0, :, 1, :n] = co[:n].T, -si[:n].T
        inverse[0, 0, :, 0, 0] = 0.5
        inverse[0, 0, :, 1, 0] = 0.5 * (-1.0) ** c0[0]
        phase = 2 * np.pi / K * ((n + ROOT * k2[:n]) * c0 % K)
        co, si = np.cos(phase), np.sin(phase)
        second[0, 0, n:, 1], second[0, 1, n:, 1] = co, -si
        inverse[0, 1, :, 0, n:], inverse[0, 1, :, 1, n:] = co.T, -si.T
    second = second.reshape(SLOTS, BLK, BLK)
    inverse = inverse.reshape(SLOTS, BLK, BLK) / K
    return left_operand(second), left_operand(inverse)


def temporal_tables():
    s = np.arange(WIN)[:, None]
    f = np.arange(BINS)[None, :]
    angle = 2 * np.pi / WIN * (s * f % WIN)
    taper = np.sin(np.pi * (s + 0.5) / WIN)
    forward = np.concatenate([np.cos(angle), np.sin(angle)], axis=1) * taper
    weight = np.where(f == 0, 1.0, 2.0) / WIN
    backward = np.concatenate([np.cos(angle) * weight, np.sin(angle) * weight], axis=1) * taper
    return np.stack(two(forward)), np.stack(two(backward.T))


def chip_of(j):
    row, i = divmod(j, 4)
    z, q = divmod(row, 4)
    x = i if row % 2 == 0 else 3 - i
    y = q if z % 2 == 0 else 3 - q
    return x, y, z


def device_of(j, core):
    x, y, z = chip_of(j)
    return (((x // 2 * 4 + y) * 8 + z) * 2 + core) * 2 + x % 2


def permutes(windows):
    partner = [(device_of(j, c), device_of(j, 1 - c)) for j in range(windows) for c in (0, 1)]
    same, cross = [], []
    for j in range(windows - 1):
        same.append((device_of(j + 1, 0), device_of(j, 0)))
        same.append((device_of(j, 1), device_of(j + 1, 1)))
        cross.append((device_of(j + 1, 0), device_of(j, 1)))
        cross.append((device_of(j, 1), device_of(j + 1, 0)))
    return partner, same, cross


def flipped(pairs):
    return [(b, a) for a, b in pairs]


def core_index():
    return lax.rem(lax.axis_index("chan"), 2)


def split(value):
    hi = value.astype(BF16)
    return hi, (value - hi.astype(F32)).astype(BF16)


def stacked(value):
    hi, lo = split(value)
    return jnp.concatenate([hi, lo, hi], axis=0)


def dot(a, b):
    return jnp.dot(a, b, preferred_element_type=F32)


def plane_slot(b):
    j, core = divmod(b, 2)
    row, i = divmod(j, 4)
    x = i if row % 2 == 0 else 3 - i
    return x // 2, row, core, x % 2


def decimate_kernel(taps_hbm, raw_ref, out_ref, taps_ref, cur_ref, band_ref, stage_ref, in_sems, out_sems):
    planes = out_ref.shape[2]
    span = TAPS + DEC * BLK
    width = raw_ref.shape[1] // planes
    pair = 2
    loads = []
    for n in range(planes // pair):
        part = pl.ds(n * pair * width, pair * width)
        loads.append(pltpu.make_async_copy(raw_ref.at[:, part], cur_ref.at[:, part], in_sems.at[n]))
        loads[-1].start()
        if n == 0:
            taps_load = pltpu.make_async_copy(taps_hbm, taps_ref, in_sems.at[planes])
            taps_load.start()
    taps_load.wait()

    i = lax.broadcasted_iota(jnp.int32, (TAPS, TAPS), 0)
    j = lax.broadcasted_iota(jnp.int32, (TAPS, TAPS), 1)
    mirror = (i + j == TAPS - 1).astype(BF16)
    rows = jnp.broadcast_to(taps_ref[...].astype(F32), (BLK, TAPS))
    mirrored = dot(rows.astype(BF16), mirror)
    wide = jnp.concatenate([mirrored, jnp.zeros((BLK, span - TAPS), F32)], axis=1)
    wide = pltpu.roll(wide, 1, 1, stride=DEC, stride_axis=0)
    band_ref[...] = wide.T.astype(BF16)

    blocks = width // (DEC * BLK)
    group = 16
    band = band_ref[...]
    stores = []
    for plane in range(planes):
        if plane % pair == 0:
            loads[plane // pair].wait()
        for b0 in range(0, blocks, group):
            spans = []
            for b in range(b0, b0 + group):
                start = plane * width + b * DEC * BLK
                if start == 0:
                    tail = jnp.zeros((cur_ref.shape[0], TAPS), BF16)
                    spans.append(jnp.concatenate([tail, cur_ref[:, : DEC * BLK]], axis=1))
                else:
                    spans.append(cur_ref[:, start - TAPS : start + DEC * BLK])
            result = dot(jnp.concatenate(spans, axis=0), band)
            for n in range(group):
                xh, row, core, xl = plane_slot(b0 + n)
                y = row if plane % 2 == 0 else 3 - row
                stage_ref[plane, xh, y, core, xl] = result[n * 16 : (n + 1) * 16]
        stores.append(pltpu.make_async_copy(stage_ref.at[plane], out_ref.at[:, :, plane], out_sems.at[plane]))
        stores[-1].start()
    for store in stores:
        store.wait()


def decimate(raw, taps):
    channels, length = raw.shape
    planes = 8
    return pl.pallas_call(
        decimate_kernel,
        in_specs=[ANY, ANY],
        out_specs=ANY,
        out_shape=jax.ShapeDtypeStruct((2, 4, planes, 2, 2, channels, BLK), F32),
        scratch_shapes=[
            pltpu.VMEM((1, TAPS), BF16),
            pltpu.VMEM(raw.shape, BF16),
            pltpu.VMEM((TAPS + DEC * BLK, BLK), BF16),
            pltpu.VMEM((planes, 2, 4, 2, 2, channels, BLK), F32),
            pltpu.SemaphoreType.DMA((planes + 1,)),
            pltpu.SemaphoreType.DMA((planes,)),
        ],
        compiler_params=params(60),
        name="decimate",
    )(taps.reshape(1, TAPS), raw)


def unplane_kernel(in_ref, out_ref):
    planes = in_ref.shape[2]
    for plane in range(planes):
        for b in range(32):
            xh, row, core, xl = plane_slot(b)
            y = row if plane % 2 == 0 else 3 - row
            start = (plane * 32 + b) * BLK
            out_ref[:, start : start + BLK] = in_ref[xh, y, plane, core, xl]


def unplane(blocks):
    planes = blocks.shape[2]
    channels = blocks.shape[5]
    return pl.pallas_call(
        unplane_kernel,
        in_specs=[VMEM],
        out_specs=VMEM,
        out_shape=jax.ShapeDtypeStruct((channels, planes * 32 * BLK), F32),
        compiler_params=params(8),
        name="unplane",
    )(blocks)


def turn(value, k, n):
    re, im = value
    if 8 * abs(k) == n:
        c = np.float32(np.sqrt(0.5))
        return ((re - im) * c, (re + im) * c) if k > 0 else ((re + im) * c, (im - re) * c)
    c, s = np.float32(np.cos(2 * np.pi * k / n)), np.float32(np.sin(2 * np.pi * k / n))
    return re * c - im * s, re * s + im * c


def real_forward(load, n, start, step):
    if n == 2:
        a, b = load(start), load(start + step)
        return [a + b, a - b]
    even = real_forward(load, n // 2, start, 2 * step)
    odd = real_forward(load, n // 2, start + step, 2 * step)
    half, quarter = n // 2, n // 4
    out = [None] * (half + 1)
    out[0], out[half] = even[0] + odd[0], even[0] - odd[0]
    out[quarter] = (even[quarter], -odd[quarter])
    for k in range(1, quarter):
        re, im = turn(odd[k], -k, n)
        er, ei = even[k]
        out[k] = (er + re, ei + im)
        out[half - k] = (er - re, im - ei)
    return out


def real_inverse(bins):
    half = len(bins) - 1
    if half == 1:
        return [bins[0] + bins[1], bins[0] - bins[1]]
    n, quarter = 2 * half, half // 2
    even, odd = [bins[0] + bins[half]], [bins[0] - bins[half]]
    for k in range(1, quarter):
        (ar, ai), (br, bi) = bins[k], bins[half - k]
        even.append((ar + br, ai - bi))
        odd.append(turn((ar - br, ai + bi), k, n))
    re, im = bins[quarter]
    even.append(re + re)
    odd.append(-(im + im))
    out = [None] * n
    out[0::2], out[1::2] = real_inverse(even), real_inverse(odd)
    return out


def real_slot(core, chunk, i):
    s = chunk * WIDTH + i % WIDTH + (HALF if i >= WIDTH else 0)
    return lax.rem(s + HALF * core, SLOTS)


def second_stage(core, chunk, mid_ref, second_ref, own_ref, other_ref):
    for i in range(PART):
        s = real_slot(core, chunk, i)
        wave = dot(second_ref[s], stacked(mid_ref[s]))
        if i < WIDTH:
            own_ref[i] = wave
        else:
            other_ref[i - WIDTH] = wave


def forward_kernel(x_hbm, second_ref, own_ref, other_ref, mid_ref, x_ref, sems):
    half = ROOT // 2
    loads = []
    for n in range(2):
        part = pl.ds(n * half, half)
        loads.append(pltpu.make_async_copy(x_hbm.at[:, part], x_ref.at[:, part], sems.at[n]))
        loads[-1].start()

    def tile(t, carry):
        rows = pl.ds(pl.multiple_of(t * 8, 8), 8)
        rows_im = pl.ds(pl.multiple_of(ROOT + t * 8, 8), 8)
        bins = real_forward(lambda c1: x_ref[c1, rows, :], ROOT, 0, 1)
        mid_ref[0, rows, :] = bins[0]
        mid_ref[0, rows_im, :] = bins[SLOTS]
        for s in range(1, SLOTS):
            mid_ref[s, rows, :], mid_ref[s, rows_im, :] = bins[s]
        return carry

    for n in range(2):
        loads[n].wait()
        lax.fori_loop(n * half // 8, (n + 1) * half // 8, tile, 0)
    second_stage(core_index(), 0, mid_ref, second_ref, own_ref, other_ref)


def forward_space(x, second):
    return pl.pallas_call(
        forward_kernel,
        in_specs=[ANY, VMEM],
        out_specs=[VMEM] * 3,
        out_shape=[WAVE, WAVE, jax.ShapeDtypeStruct((SLOTS, BLK, BLK), F32)],
        scratch_shapes=[pltpu.VMEM((ROOT, ROOT, BLK), F32), pltpu.SemaphoreType.DMA((2,))],
        compiler_params=params(14),
        name="forward_space",
    )(x.reshape(ROOT, ROOT, BLK), second)


def forward_more_kernel(chunk, mid_ref, second_ref, own_ref, other_ref):
    second_stage(core_index(), chunk, mid_ref, second_ref, own_ref, other_ref)


def forward_more(chunk, middle, second):
    return pl.pallas_call(
        functools.partial(forward_more_kernel, chunk),
        in_specs=[VMEM] * 2,
        out_specs=[VMEM] * 2,
        out_shape=[WAVE, WAVE],
        compiler_params=params(12),
        name="forward_more",
    )(middle, second)


def inverse_stage(core, chunk, own_ref, halo_ref, part_ref, cross_ref, inv_ref, mid_ref):
    for i in range(PART):
        if i < WIDTH:
            z = own_ref[i] + halo_ref[i]
        else:
            z = part_ref[i - WIDTH] + cross_ref[i - WIDTH]
        mid_ref[i] = dot(inv_ref[real_slot(core, chunk, i)], stacked(z))


def inverse_more_kernel(chunk, own_ref, halo_ref, part_ref, cross_ref, inv_ref, mid_ref):
    inverse_stage(core_index(), chunk, own_ref, halo_ref, part_ref, cross_ref, inv_ref, mid_ref)


def inverse_more(chunk, waves, inv):
    return pl.pallas_call(
        functools.partial(inverse_more_kernel, chunk),
        in_specs=[VMEM] * 5,
        out_specs=VMEM,
        out_shape=MIDDLE,
        compiler_params=params(12),
        name="inverse_more",
    )(*waves, inv)


def inverse_kernel(own_ref, halo_ref, part_ref, cross_ref, inv_ref, *rest):
    earlier, out_ref, mid_ref = rest[:-2], rest[-2], rest[-1]
    core = core_index()
    inverse_stage(core, CHUNKS - 1, own_ref, halo_ref, part_ref, cross_ref, inv_ref, mid_ref)
    refs = earlier + (mid_ref,)

    def tile(t, carry):
        rows = pl.ds(pl.multiple_of(t * 8, 8), 8)
        rows_im = pl.ds(pl.multiple_of(ROOT + t * 8, 8), 8)

        def both(s):
            ref = refs[s % HALF // WIDTH]
            place = s % WIDTH + WIDTH * lax.rem(core + s // HALF, 2)
            return ref[place, rows, :], ref[place, rows_im, :]

        low, high = both(0)
        values = real_inverse([low] + [both(s) for s in range(1, SLOTS)] + [high])
        for c1 in range(ROOT):
            out_ref[c1, rows, :] = values[c1]
        return carry

    lax.fori_loop(0, ROOT // 8, tile, 0)


def inverse_space(waves, earlier, inv):
    return pl.pallas_call(
        inverse_kernel,
        in_specs=[VMEM] * (5 + len(earlier)),
        out_specs=VMEM,
        out_shape=jax.ShapeDtypeStruct((ROOT, ROOT, BLK), F32),
        scratch_shapes=[pltpu.VMEM(MIDDLE.shape, F32)],
        compiler_params=params(14),
        name="inverse_space",
    )(*waves, inv, *earlier)


def gains_kernel(gain_ref, band_ref, out_ref):
    core = core_index()
    n = ROOT // 2
    i = lax.broadcasted_iota(jnp.int32, (ROOT, ROOT), 0)
    j = lax.broadcasted_iota(jnp.int32, (ROOT, ROOT), 1)
    mirror = (i + j == ROOT - 1).astype(BF16)
    source = jnp.where(i == 0, 0, jnp.where(i < n, n - i, n + ROOT - 1 - i))
    mirror0 = (j == source).astype(BF16)

    def rows(k1, k2, count):
        return band_ref[pl.ds(k1 + ROOT * k2, count, stride=ROOT), :]

    def exact(perm, bands):
        return dot(perm, bands.astype(F32).astype(BF16))

    def pick(bands):
        total = jnp.zeros(bands.shape, F32)
        for b in range(BANDS):
            total = jnp.where(bands == b, gain_ref[b], total)
        return total

    def put(s, plus, minus):
        gp, gm = pick(plus.astype(F32)), pick(minus)
        out_ref[0, s] = gp + gm
        out_ref[1, s] = gp - gm

    for s in range(HALF):
        if s:
            k1 = s + HALF * core
            put(s, rows(k1, 0, ROOT), exact(mirror, rows(ROOT - k1, 0, ROOT)))
            continue

        @pl.when(core == 0)
        def _():
            plus = jnp.concatenate([rows(0, 0, n), rows(n, 0, n)], axis=0)
            minus = jnp.concatenate([rows(0, n, n), rows(n, n, n)], axis=0)
            put(0, plus, exact(mirror0, minus))

        @pl.when(core != 0)
        def _():
            put(0, rows(HALF, 0, ROOT), exact(mirror, rows(ROOT - HALF, 0, ROOT)))


def gains(band_gain, fan_band):
    return pl.pallas_call(
        gains_kernel,
        in_specs=[SMEM, VMEM],
        out_specs=VMEM,
        out_shape=jax.ShapeDtypeStruct((2, HALF, ROOT, BLK), F32),
        compiler_params=params(8),
        name="gains",
    )(band_gain, fan_band)


def time_kernel(first_chunk, *refs):
    own_ref, part_ref, same_ref, cross_ref, mine_ref, theirs_ref, fwd_ref, bwd_ref = refs[:8]
    out_refs = refs[8:]
    core, xl = core_index(), lax.axis_index("tile")
    step = pl.program_id(0)
    slots = own_ref.shape[0]
    rows = slots * BLK
    even = core == 0

    def flat(ref):
        return ref[...].reshape(rows, BLK)

    own, part, same, cross = flat(own_ref), flat(part_ref), flat(same_ref), flat(cross_ref)
    x = jnp.concatenate(
        [
            jnp.where(even, cross, same),
            jnp.where(even, own, part),
            jnp.where(even, part, own),
            jnp.where(even, same, cross),
        ],
        axis=1,
    )
    hi, lo = split(x)
    fwd_hi = fwd_ref[0]
    v = dot(hi, fwd_hi) + dot(lo, fwd_hi) + dot(hi, fwd_ref[1])
    pieces = []
    for s in range(slots):
        p = v[s * BLK : s * BLK + ROOT]
        q = v[s * BLK + ROOT : (s + 1) * BLK]
        a, d = p[:, :BINS], p[:, BINS:]
        c, b = q[:, :BINS], q[:, BINS:]

        def wide(kind):
            mine, theirs = mine_ref[kind, s], theirs_ref[kind, s]
            low = jnp.where(xl == 0, mine, theirs)
            high = jnp.where(xl == 0, theirs, mine)
            return jnp.concatenate([low, high], axis=1)

        gs, gd = wide(0), wide(1)
        gr = gi = gs
        if s == 0 and first_chunk:
            row = lax.broadcasted_iota(jnp.int32, (ROOT, BINS), 0)
            pair = (row == 0) & (step == 0) & even
            gr = jnp.where(pair, gs + gd, gs)
            gi = jnp.where(pair, gs - gd, gs)
            gd = jnp.where(pair, 0.0, gd)
        pieces.append(jnp.concatenate([gr * a + gd * b, gr * d - gd * c], axis=1))
        pieces.append(jnp.concatenate([gi * c - gd * d, gd * a + gi * b], axis=1))
    hi, lo = split(jnp.concatenate(pieces, axis=0))
    bwd_hi = bwd_ref[0]
    z = dot(hi, bwd_hi) + dot(lo, bwd_hi) + dot(hi, bwd_ref[1])
    before, low, high, after = (z[:, n * BLK : (n + 1) * BLK] for n in range(4))
    outs = [
        jnp.where(even, low, high),
        jnp.where(even, high, low),
        jnp.where(even, after, before),
        jnp.where(even, before, after),
    ]
    for out_ref, value in zip(out_refs, outs):
        out_ref[...] = value.reshape(slots, BLK, BLK)


def time_filter(chunk, waves, mine, theirs, fwd, bwd):
    slots = 8
    steps = WIDTH // slots
    data = pl.BlockSpec((slots, BLK, BLK), lambda g: (g, 0, 0))
    gain = pl.BlockSpec((2, slots, ROOT, BLK), lambda g: (0, chunk * steps + g, 0, 0))
    table = pl.BlockSpec((2, WIN, WIN), lambda g: (0, 0, 0))
    return pl.pallas_call(
        functools.partial(time_kernel, chunk == 0),
        grid=(steps,),
        in_specs=[data] * 4 + [gain] * 2 + [table] * 2,
        out_specs=[data] * 4,
        out_shape=[jax.ShapeDtypeStruct((WIDTH, BLK, BLK), F32)] * 4,
        compiler_params=params(24),
        name="time_filter",
    )(*waves, mine, theirs, fwd, bwd)


def body(raw_strain, fir_taps, fan_band, band_gain):
    second, inverse = (jnp.asarray(t) for t in spatial_tables())
    fwd, bwd = (jnp.asarray(t) for t in temporal_tables())
    partner, same, cross = permutes(raw_strain.shape[1] // DEC // HOP)

    mine = gains(band_gain, fan_band)
    theirs = lax.ppermute(mine, "tile", [(0, 1), (1, 0)])

    blocks = decimate(raw_strain, fir_taps)
    shape = blocks.shape
    blocks = blocks.reshape((256,) + shape[5:])
    blocks = lax.all_to_all(blocks, AXES, 0, 0, tiled=True)
    own, other, middle = forward_space(blocks, second)
    received = []
    for g in range(CHUNKS):
        if g:
            own, other = forward_more(g, middle, second)
        from_partner = lax.ppermute(other, AXES, partner)
        from_same = lax.ppermute(own, AXES, same)
        from_cross = lax.ppermute(other, AXES, cross)
        received.append((own, from_partner, from_same, from_cross))
    returned = []
    for g in range(CHUNKS):
        own, part, halo, far = time_filter(g, received[g], mine, theirs, fwd, bwd)
        back_partner = lax.ppermute(part, AXES, partner)
        back_same = lax.ppermute(halo, AXES, flipped(same))
        back_cross = lax.ppermute(far, AXES, flipped(cross))
        returned.append((own, back_same, back_partner, back_cross))
    earlier = [inverse_more(g, returned[g], inverse) for g in range(CHUNKS - 1)]
    filtered = inverse_space(returned[-1], earlier, inverse)
    filtered = lax.all_to_all(filtered.reshape(256, 16, BLK), AXES, 0, 0, tiled=True)
    return unplane(filtered.reshape(shape))


def solution(mesh):
    return jax.shard_map(
        body,
        mesh=mesh,
        in_specs=(P(AXES, None), P(), P(None, "tile"), P()),
        out_specs=P(AXES, None),
        check_vma=False,
    )
```

```python
import functools

import jax
import jax.numpy as jnp
import numpy as np
from jax import lax
from jax.experimental import pallas as pl
from jax.experimental.pallas import tpu as pltpu
from jax.sharding import PartitionSpec as P
import ml_dtypes

K = 4096
ROOT = 64
WIN = 512
TAPS = 128
DEC = 4
BANDS = 8
HOP = 256
BINS = 256
BLK = 128
SLOTS = 32
HALF = 16
CHUNKS = 2
WIDTH = HALF // CHUNKS
PART = 2 * WIDTH
AXES = ("chan", "tile")
F32 = jnp.float32
BF16 = jnp.bfloat16
MIB = 1024 * 1024
WAVE = jax.ShapeDtypeStruct((WIDTH, BLK, BLK), F32)
MIDDLE = jax.ShapeDtypeStruct((PART, BLK, BLK), F32)


def params(mib):
    return pltpu.CompilerParams(vmem_limit_bytes=mib * MIB)


VMEM = pl.BlockSpec(memory_space=pltpu.VMEM)
SMEM = pl.BlockSpec(memory_space=pltpu.SMEM)
ANY = pl.BlockSpec(memory_space=pl.ANY)


def two(table):
    table = np.asarray(table, np.float32)
    hi = table.astype(ml_dtypes.bfloat16)
    lo = (table - hi.astype(np.float32)).astype(ml_dtypes.bfloat16)
    return hi, lo


def left_operand(table):
    hi, lo = two(table)
    return np.concatenate([hi, hi, lo], axis=-1)


def spatial_tables():
    c0 = np.arange(ROOT)[None, :]
    k2 = np.arange(ROOT)[:, None]
    second = np.zeros((SLOTS, 2, ROOT, 2, ROOT))
    inverse = np.zeros((SLOTS, 2, ROOT, 2, ROOT))
    for s in range(SLOTS):
        phase = 2 * np.pi / K * ((s + ROOT * k2) * c0 % K)
        co, si = np.cos(phase), np.sin(phase)
        if s:
            second[s, 0, :, 0], second[s, 0, :, 1] = co, si
            second[s, 1, :, 0], second[s, 1, :, 1] = -si, co
            inverse[s, 0, :, 0], inverse[s, 0, :, 1] = co.T / 2, -si.T / 2
            inverse[s, 1, :, 0], inverse[s, 1, :, 1] = si.T / 2, co.T / 2
            continue
        n = ROOT // 2
        second[0, 0, :n, 0], second[0, 1, :n, 0] = co[:n], -si[:n]
        second[0, 1, 0, 0] = (-1.0) ** c0[0]
        inverse[0, 0, :, 0, :n], inverse[0, 0, :, 1, :n] = co[:n].T, -si[:n].T
        inverse[0, 0, :, 0, 0] = 0.5
        inverse[0, 0, :, 1, 0] = 0.5 * (-1.0) ** c0[0]
        phase = 2 * np.pi / K * ((n + ROOT * k2[:n]) * c0 % K)
        co, si = np.cos(phase), np.sin(phase)
        second[0, 0, n:, 1], second[0, 1, n:, 1] = co, -si
        inverse[0, 1, :, 0, n:], inverse[0, 1, :, 1, n:] = co.T, -si.T
    second = second.reshape(SLOTS, BLK, BLK)
    inverse = inverse.reshape(SLOTS, BLK, BLK) / K
    return left_operand(second), left_operand(inverse)


def temporal_tables():
    s = np.arange(WIN)[:, None]
    f = np.arange(BINS)[None, :]
    angle = 2 * np.pi / WIN * (s * f % WIN)
    taper = np.sin(np.pi * (s + 0.5) / WIN)
    forward = np.concatenate([np.cos(angle), np.sin(angle)], axis=1) * taper
    weight = np.where(f == 0, 1.0, 2.0) / WIN
    backward = np.concatenate([np.cos(angle) * weight, np.sin(angle) * weight], axis=1) * taper
    return np.stack(two(forward)), np.stack(two(backward.T))


def chip_of(j):
    row, i = divmod(j, 4)
    z, q = divmod(row, 4)
    x = i if row % 2 == 0 else 3 - i
    y = q if z % 2 == 0 else 3 - q
    return x, y, z


def device_of(j, core):
    x, y, z = chip_of(j)
    return (((x // 2 * 4 + y) * 8 + z) * 2 + core) * 2 + x % 2


def permutes(windows):
    partner = [(device_of(j, c), device_of(j, 1 - c)) for j in range(windows) for c in (0, 1)]
    same, cross = [], []
    for j in range(windows - 1):
        same.append((device_of(j + 1, 0), device_of(j, 0)))
        same.append((device_of(j, 1), device_of(j + 1, 1)))
        cross.append((device_of(j + 1, 0), device_of(j, 1)))
        cross.append((device_of(j, 1), device_of(j + 1, 0)))
    return partner, same, cross


def flipped(pairs):
    return [(b, a) for a, b in pairs]


def core_index():
    return lax.rem(lax.axis_index("chan"), 2)


def split(value):
    hi = value.astype(BF16)
    return hi, (value - hi.astype(F32)).astype(BF16)


def stacked(value):
    hi, lo = split(value)
    return jnp.concatenate([hi, lo, hi], axis=0)


def dot(a, b):
    return jnp.dot(a, b, preferred_element_type=F32)


def plane_slot(b):
    j, core = divmod(b, 2)
    row, i = divmod(j, 4)
    x = i if row % 2 == 0 else 3 - i
    return x // 2, row, core, x % 2


def decimate_kernel(taps_hbm, raw_ref, out_ref, taps_ref, cur_ref, band_ref, stage_ref, in_sems, out_sems):
    planes = out_ref.shape[2]
    span = TAPS + DEC * BLK
    width = raw_ref.shape[1] // planes
    pair = 2
    loads = []
    for n in range(planes // pair):
        part = pl.ds(n * pair * width, pair * width)
        loads.append(pltpu.make_async_copy(raw_ref.at[:, part], cur_ref.at[:, part], in_sems.at[n]))
        loads[-1].start()
        if n == 0:
            taps_load = pltpu.make_async_copy(taps_hbm, taps_ref, in_sems.at[planes])
            taps_load.start()
    taps_load.wait()

    i = lax.broadcasted_iota(jnp.int32, (TAPS, TAPS), 0)
    j = lax.broadcasted_iota(jnp.int32, (TAPS, TAPS), 1)
    mirror = (i + j == TAPS - 1).astype(BF16)
    rows = jnp.broadcast_to(taps_ref[...].astype(F32), (BLK, TAPS))
    mirrored = dot(rows.astype(BF16), mirror)
    wide = jnp.concatenate([mirrored, jnp.zeros((BLK, span - TAPS), F32)], axis=1)
    wide = pltpu.roll(wide, 1, 1, stride=DEC, stride_axis=0)
    band_ref[...] = wide.T.astype(BF16)

    blocks = width // (DEC * BLK)
    group = 16
    band = band_ref[...]
    stores = []
    for plane in range(planes):
        if plane % pair == 0:
            loads[plane // pair].wait()
        for b0 in range(0, blocks, group):
            spans = []
            for b in range(b0, b0 + group):
                start = plane * width + b * DEC * BLK
                if start == 0:
                    tail = jnp.zeros((cur_ref.shape[0], TAPS), BF16)
                    spans.append(jnp.concatenate([tail, cur_ref[:, : DEC * BLK]], axis=1))
                else:
                    spans.append(cur_ref[:, start - TAPS : start + DEC * BLK])
            result = dot(jnp.concatenate(spans, axis=0), band)
            for n in range(group):
                xh, row, core, xl = plane_slot(b0 + n)
                y = row if plane % 2 == 0 else 3 - row
                stage_ref[plane, xh, y, core, xl] = result[n * 16 : (n + 1) * 16]
        stores.append(pltpu.make_async_copy(stage_ref.at[plane], out_ref.at[:, :, plane], out_sems.at[plane]))
        stores[-1].start()
    for store in stores:
        store.wait()


def decimate(raw, taps):
    channels, length = raw.shape
    planes = 8
    return pl.pallas_call(
        decimate_kernel,
        in_specs=[ANY, ANY],
        out_specs=ANY,
        out_shape=jax.ShapeDtypeStruct((2, 4, planes, 2, 2, channels, BLK), F32),
        scratch_shapes=[
            pltpu.VMEM((1, TAPS), BF16),
            pltpu.VMEM(raw.shape, BF16),
            pltpu.VMEM((TAPS + DEC * BLK, BLK), BF16),
            pltpu.VMEM((planes, 2, 4, 2, 2, channels, BLK), F32),
            pltpu.SemaphoreType.DMA((planes + 1,)),
            pltpu.SemaphoreType.DMA((planes,)),
        ],
        compiler_params=params(60),
        name="decimate",
    )(taps.reshape(1, TAPS), raw)


def unplane_kernel(in_ref, out_ref, stage_ref, sems):
    planes = in_ref.shape[2]
    pair = 2
    stores = []
    for plane in range(planes):
        for b in range(32):
            xh, row, core, xl = plane_slot(b)
            y = row if plane % 2 == 0 else 3 - row
            start = (plane * 32 + b) * BLK
            stage_ref[:, start : start + BLK] = in_ref[xh, y, plane, core, xl]
        if plane % pair == pair - 1:
            part = pl.ds((plane + 1 - pair) * 32 * BLK, pair * 32 * BLK)
            store = pltpu.make_async_copy(stage_ref.at[:, part], out_ref.at[:, part], sems.at[plane // pair])
            store.start()
            stores.append(store)
    for store in stores:
        store.wait()


def unplane(blocks):
    planes = blocks.shape[2]
    channels = blocks.shape[5]
    return pl.pallas_call(
        unplane_kernel,
        in_specs=[VMEM],
        out_specs=ANY,
        out_shape=jax.ShapeDtypeStruct((channels, planes * 32 * BLK), F32),
        scratch_shapes=[
            pltpu.VMEM((channels, planes * 32 * BLK), F32),
            pltpu.SemaphoreType.DMA((planes // 2,)),
        ],
        compiler_params=params(8),
        name="unplane",
    )(blocks)


def turn(value, k, n):
    re, im = value
    if 8 * abs(k) == n:
        c = np.float32(np.sqrt(0.5))
        return ((re - im) * c, (re + im) * c) if k > 0 else ((re + im) * c, (im - re) * c)
    c, s = np.float32(np.cos(2 * np.pi * k / n)), np.float32(np.sin(2 * np.pi * k / n))
    return re * c - im * s, re * s + im * c


def real_forward(load, n, start, step):
    if n == 2:
        a, b = load(start), load(start + step)
        return [a + b, a - b]
    even = real_forward(load, n // 2, start, 2 * step)
    odd = real_forward(load, n // 2, start + step, 2 * step)
    half, quarter = n // 2, n // 4
    out = [None] * (half + 1)
    out[0], out[half] = even[0] + odd[0], even[0] - odd[0]
    out[quarter] = (even[quarter], -odd[quarter])
    for k in range(1, quarter):
        re, im = turn(odd[k], -k, n)
        er, ei = even[k]
        out[k] = (er + re, ei + im)
        out[half - k] = (er - re, im - ei)
    return out


def real_inverse(bins):
    half = len(bins) - 1
    if half == 1:
        return [bins[0] + bins[1], bins[0] - bins[1]]
    n, quarter = 2 * half, half // 2
    even, odd = [bins[0] + bins[half]], [bins[0] - bins[half]]
    for k in range(1, quarter):
        (ar, ai), (br, bi) = bins[k], bins[half - k]
        even.append((ar + br, ai - bi))
        odd.append(turn((ar - br, ai + bi), k, n))
    re, im = bins[quarter]
    even.append(re + re)
    odd.append(-(im + im))
    out = [None] * n
    out[0::2], out[1::2] = real_inverse(even), real_inverse(odd)
    return out


def real_slot(core, chunk, i):
    s = chunk * WIDTH + i % WIDTH + (HALF if i >= WIDTH else 0)
    return lax.rem(s + HALF * core, SLOTS)


def second_stage(core, chunk, mid_ref, second_ref, own_ref, other_ref):
    for i in range(PART):
        s = real_slot(core, chunk, i)
        wave = dot(second_ref[s], stacked(mid_ref[s]))
        if i < WIDTH:
            own_ref[i] = wave
        else:
            other_ref[i - WIDTH] = wave


def forward_kernel(x_hbm, second_ref, own_ref, other_ref, mid_ref, x_ref, sems):
    half = ROOT // 2
    loads = []
    for n in range(2):
        part = pl.ds(n * half, half)
        loads.append(pltpu.make_async_copy(x_hbm.at[:, part], x_ref.at[:, part], sems.at[n]))
        loads[-1].start()

    def tile(t, carry):
        rows = pl.ds(pl.multiple_of(t * 8, 8), 8)
        rows_im = pl.ds(pl.multiple_of(ROOT + t * 8, 8), 8)
        bins = real_forward(lambda c1: x_ref[c1, rows, :], ROOT, 0, 1)
        mid_ref[0, rows, :] = bins[0]
        mid_ref[0, rows_im, :] = bins[SLOTS]
        for s in range(1, SLOTS):
            mid_ref[s, rows, :], mid_ref[s, rows_im, :] = bins[s]
        return carry

    for n in range(2):
        loads[n].wait()
        lax.fori_loop(n * half // 8, (n + 1) * half // 8, tile, 0)
    second_stage(core_index(), 0, mid_ref, second_ref, own_ref, other_ref)


def forward_space(x, second):
    return pl.pallas_call(
        forward_kernel,
        in_specs=[ANY, VMEM],
        out_specs=[VMEM] * 3,
        out_shape=[WAVE, WAVE, jax.ShapeDtypeStruct((SLOTS, BLK, BLK), F32)],
        scratch_shapes=[pltpu.VMEM((ROOT, ROOT, BLK), F32), pltpu.SemaphoreType.DMA((2,))],
        compiler_params=params(14),
        name="forward_space",
    )(x.reshape(ROOT, ROOT, BLK), second)


def forward_more_kernel(chunk, mid_ref, second_ref, own_ref, other_ref):
    second_stage(core_index(), chunk, mid_ref, second_ref, own_ref, other_ref)


def forward_more(chunk, middle, second):
    return pl.pallas_call(
        functools.partial(forward_more_kernel, chunk),
        in_specs=[VMEM] * 2,
        out_specs=[VMEM] * 2,
        out_shape=[WAVE, WAVE],
        compiler_params=params(12),
        name="forward_more",
    )(middle, second)


def inverse_stage(core, chunk, own_ref, halo_ref, part_ref, cross_ref, inv_ref, mid_ref):
    for i in range(PART):
        if i < WIDTH:
            z = own_ref[i] + halo_ref[i]
        else:
            z = part_ref[i - WIDTH] + cross_ref[i - WIDTH]
        mid_ref[i] = dot(inv_ref[real_slot(core, chunk, i)], stacked(z))


def inverse_more_kernel(chunk, own_ref, halo_ref, part_ref, cross_ref, inv_ref, mid_ref):
    inverse_stage(core_index(), chunk, own_ref, halo_ref, part_ref, cross_ref, inv_ref, mid_ref)


def inverse_more(chunk, waves, inv):
    return pl.pallas_call(
        functools.partial(inverse_more_kernel, chunk),
        in_specs=[VMEM] * 5,
        out_specs=VMEM,
        out_shape=MIDDLE,
        compiler_params=params(12),
        name="inverse_more",
    )(*waves, inv)


def inverse_kernel(own_ref, halo_ref, part_ref, cross_ref, inv_ref, *rest):
    earlier, out_ref, mid_ref = rest[:-2], rest[-2], rest[-1]
    core = core_index()
    inverse_stage(core, CHUNKS - 1, own_ref, halo_ref, part_ref, cross_ref, inv_ref, mid_ref)
    refs = earlier + (mid_ref,)

    def tile(t, carry):
        rows = pl.ds(pl.multiple_of(t * 8, 8), 8)
        rows_im = pl.ds(pl.multiple_of(ROOT + t * 8, 8), 8)

        def both(s):
            ref = refs[s % HALF // WIDTH]
            place = s % WIDTH + WIDTH * lax.rem(core + s // HALF, 2)
            return ref[place, rows, :], ref[place, rows_im, :]

        low, high = both(0)
        values = real_inverse([low] + [both(s) for s in range(1, SLOTS)] + [high])
        for c1 in range(ROOT):
            out_ref[c1, rows, :] = values[c1]
        return carry

    lax.fori_loop(0, ROOT // 8, tile, 0)


def inverse_space(waves, earlier, inv):
    return pl.pallas_call(
        inverse_kernel,
        in_specs=[VMEM] * (5 + len(earlier)),
        out_specs=VMEM,
        out_shape=jax.ShapeDtypeStruct((ROOT, ROOT, BLK), F32),
        scratch_shapes=[pltpu.VMEM(MIDDLE.shape, F32)],
        compiler_params=params(14),
        name="inverse_space",
    )(*waves, inv, *earlier)


def gains_kernel(gain_ref, band_ref, out_ref):
    core = core_index()
    n = ROOT // 2
    i = lax.broadcasted_iota(jnp.int32, (ROOT, ROOT), 0)
    j = lax.broadcasted_iota(jnp.int32, (ROOT, ROOT), 1)
    mirror = (i + j == ROOT - 1).astype(BF16)
    source = jnp.where(i == 0, 0, jnp.where(i < n, n - i, n + ROOT - 1 - i))
    mirror0 = (j == source).astype(BF16)

    def rows(k1, k2, count):
        return band_ref[pl.ds(k1 + ROOT * k2, count, stride=ROOT), :]

    def exact(perm, bands):
        return dot(perm, bands.astype(F32).astype(BF16))

    def pick(bands):
        total = jnp.zeros(bands.shape, F32)
        for b in range(BANDS):
            total = jnp.where(bands == b, gain_ref[b], total)
        return total

    def put(s, plus, minus):
        gp, gm = pick(plus.astype(F32)), pick(minus)
        out_ref[0, s] = gp + gm
        out_ref[1, s] = gp - gm

    for s in range(HALF):
        if s:
            k1 = s + HALF * core
            put(s, rows(k1, 0, ROOT), exact(mirror, rows(ROOT - k1, 0, ROOT)))
            continue

        @pl.when(core == 0)
        def _():
            plus = jnp.concatenate([rows(0, 0, n), rows(n, 0, n)], axis=0)
            minus = jnp.concatenate([rows(0, n, n), rows(n, n, n)], axis=0)
            put(0, plus, exact(mirror0, minus))

        @pl.when(core != 0)
        def _():
            put(0, rows(HALF, 0, ROOT), exact(mirror, rows(ROOT - HALF, 0, ROOT)))


def gains(band_gain, fan_band):
    return pl.pallas_call(
        gains_kernel,
        in_specs=[SMEM, VMEM],
        out_specs=VMEM,
        out_shape=jax.ShapeDtypeStruct((2, HALF, ROOT, BLK), F32),
        compiler_params=params(8),
        name="gains",
    )(band_gain, fan_band)


def time_kernel(chunk, *refs):
    own_ref, part_ref, same_ref, cross_ref, mine_ref, theirs_ref, fwd_ref, bwd_ref = refs[:8]
    out_refs = refs[8:]
    core, xl = core_index(), lax.axis_index("tile")
    slots = own_ref.shape[0]
    rows = slots * BLK
    even = core == 0

    def flat(ref):
        return ref[...].reshape(rows, BLK)

    own, part, same, cross = flat(own_ref), flat(part_ref), flat(same_ref), flat(cross_ref)
    x = jnp.concatenate(
        [
            jnp.where(even, cross, same),
            jnp.where(even, own, part),
            jnp.where(even, part, own),
            jnp.where(even, same, cross),
        ],
        axis=1,
    )
    hi, lo = split(x)
    fwd_hi = fwd_ref[0]
    v = dot(hi, fwd_hi) + dot(lo, fwd_hi) + dot(hi, fwd_ref[1])
    pieces = []
    for s in range(slots):
        p = v[s * BLK : s * BLK + ROOT]
        q = v[s * BLK + ROOT : (s + 1) * BLK]
        a, d = p[:, :BINS], p[:, BINS:]
        c, b = q[:, :BINS], q[:, BINS:]

        def wide(kind):
            place = chunk * WIDTH + s
            mine, theirs = mine_ref[kind, place], theirs_ref[kind, place]
            low = jnp.where(xl == 0, mine, theirs)
            high = jnp.where(xl == 0, theirs, mine)
            return jnp.concatenate([low, high], axis=1)

        gs, gd = wide(0), wide(1)
        gr = gi = gs
        if s == 0 and chunk == 0:
            row = lax.broadcasted_iota(jnp.int32, (ROOT, BINS), 0)
            pair = (row == 0) & even
            gr = jnp.where(pair, gs + gd, gs)
            gi = jnp.where(pair, gs - gd, gs)
            gd = jnp.where(pair, 0.0, gd)
        pieces.append(jnp.concatenate([gr * a + gd * b, gr * d - gd * c], axis=1))
        pieces.append(jnp.concatenate([gi * c - gd * d, gd * a + gi * b], axis=1))
    hi, lo = split(jnp.concatenate(pieces, axis=0))
    bwd_hi = bwd_ref[0]
    z = dot(hi, bwd_hi) + dot(lo, bwd_hi) + dot(hi, bwd_ref[1])
    before, low, high, after = (z[:, n * BLK : (n + 1) * BLK] for n in range(4))
    outs = [
        jnp.where(even, low, high),
        jnp.where(even, high, low),
        jnp.where(even, after, before),
        jnp.where(even, before, after),
    ]
    for out_ref, value in zip(out_refs, outs):
        out_ref[...] = value.reshape(slots, BLK, BLK)


def time_filter(chunk, waves, mine, theirs, fwd, bwd):
    return pl.pallas_call(
        functools.partial(time_kernel, chunk),
        in_specs=[VMEM] * 8,
        out_specs=[VMEM] * 4,
        out_shape=[WAVE] * 4,
        compiler_params=params(28),
        name="time_filter",
    )(*waves, mine, theirs, fwd, bwd)


def body(raw_strain, fir_taps, fan_band, band_gain):
    second, inverse = (jnp.asarray(t) for t in spatial_tables())
    fwd, bwd = (jnp.asarray(t) for t in temporal_tables())
    partner, same, cross = permutes(raw_strain.shape[1] // DEC // HOP)

    mine = gains(band_gain, fan_band)
    theirs = lax.ppermute(mine, "tile", [(0, 1), (1, 0)])

    blocks = decimate(raw_strain, fir_taps)
    shape = blocks.shape
    blocks = blocks.reshape((256,) + shape[5:])
    blocks = lax.all_to_all(blocks, AXES, 0, 0, tiled=True)
    own, other, middle = forward_space(blocks, second)
    received = []
    for g in range(CHUNKS):
        if g:
            own, other = forward_more(g, middle, second)
        from_partner = lax.ppermute(other, AXES, partner)
        from_same = lax.ppermute(own, AXES, same)
        from_cross = lax.ppermute(other, AXES, cross)
        received.append((own, from_partner, from_same, from_cross))
    returned = []
    for g in range(CHUNKS):
        own, part, halo, far = time_filter(g, received[g], mine, theirs, fwd, bwd)
        back_partner = lax.ppermute(part, AXES, partner)
        back_same = lax.ppermute(halo, AXES, flipped(same))
        back_cross = lax.ppermute(far, AXES, flipped(cross))
        returned.append((own, back_same, back_partner, back_cross))
    earlier = [inverse_more(g, returned[g], inverse) for g in range(CHUNKS - 1)]
    filtered = inverse_space(returned[-1], earlier, inverse)
    filtered = lax.all_to_all(filtered.reshape(256, 16, BLK), AXES, 0, 0, tiled=True)
    return unplane(filtered.reshape(shape))


def solution(mesh):
    return jax.shard_map(
        body,
        mesh=mesh,
        in_specs=(P(AXES, None), P(), P(None, "tile"), P()),
        out_specs=P(AXES, None),
        check_vma=False,
    )
```

```python
import functools

import jax
import jax.numpy as jnp
import numpy as np
from jax import lax
from jax.experimental import pallas as pl
from jax.experimental.pallas import tpu as pltpu
from jax.sharding import PartitionSpec as P
import ml_dtypes

K = 4096
ROOT = 64
WIN = 512
TAPS = 128
DEC = 4
BANDS = 8
HOP = 256
BINS = 256
BLK = 128
SLOTS = 32
HALF = 16
CHUNKS = 2
WIDTH = HALF // CHUNKS
PART = 2 * WIDTH
AXES = ("chan", "tile")
F32 = jnp.float32
BF16 = jnp.bfloat16
MIB = 1024 * 1024
WAVE = jax.ShapeDtypeStruct((WIDTH, BLK, BLK), F32)
MIDDLE = jax.ShapeDtypeStruct((PART, BLK, BLK), F32)


def params(mib):
    return pltpu.CompilerParams(vmem_limit_bytes=mib * MIB)


VMEM = pl.BlockSpec(memory_space=pltpu.VMEM)
SMEM = pl.BlockSpec(memory_space=pltpu.SMEM)
ANY = pl.BlockSpec(memory_space=pl.ANY)


def two(table):
    table = np.asarray(table, np.float32)
    hi = table.astype(ml_dtypes.bfloat16)
    lo = (table - hi.astype(np.float32)).astype(ml_dtypes.bfloat16)
    return hi, lo


def left_operand(table):
    hi, lo = two(table)
    return np.concatenate([hi, hi, lo], axis=-1)


def spatial_tables():
    c0 = np.arange(ROOT)[None, :]
    k2 = np.arange(ROOT)[:, None]
    second = np.zeros((SLOTS, 2, ROOT, 2, ROOT))
    inverse = np.zeros((SLOTS, 2, ROOT, 2, ROOT))
    for s in range(SLOTS):
        phase = 2 * np.pi / K * ((s + ROOT * k2) * c0 % K)
        co, si = np.cos(phase), np.sin(phase)
        if s:
            second[s, 0, :, 0], second[s, 0, :, 1] = co, si
            second[s, 1, :, 0], second[s, 1, :, 1] = -si, co
            inverse[s, 0, :, 0], inverse[s, 0, :, 1] = co.T / 2, -si.T / 2
            inverse[s, 1, :, 0], inverse[s, 1, :, 1] = si.T / 2, co.T / 2
            continue
        n = ROOT // 2
        second[0, 0, :n, 0], second[0, 1, :n, 0] = co[:n], -si[:n]
        second[0, 1, 0, 0] = (-1.0) ** c0[0]
        inverse[0, 0, :, 0, :n], inverse[0, 0, :, 1, :n] = co[:n].T, -si[:n].T
        inverse[0, 0, :, 0, 0] = 0.5
        inverse[0, 0, :, 1, 0] = 0.5 * (-1.0) ** c0[0]
        phase = 2 * np.pi / K * ((n + ROOT * k2[:n]) * c0 % K)
        co, si = np.cos(phase), np.sin(phase)
        second[0, 0, n:, 1], second[0, 1, n:, 1] = co, -si
        inverse[0, 1, :, 0, n:], inverse[0, 1, :, 1, n:] = co.T, -si.T
    second = second.reshape(SLOTS, BLK, BLK)
    inverse = inverse.reshape(SLOTS, BLK, BLK) / K
    return left_operand(second), left_operand(inverse)


def temporal_tables():
    s = np.arange(WIN)[:, None]
    f = np.arange(BINS)[None, :]
    angle = 2 * np.pi / WIN * (s * f % WIN)
    taper = np.sin(np.pi * (s + 0.5) / WIN)
    forward = np.concatenate([np.cos(angle), np.sin(angle)], axis=1) * taper
    weight = np.where(f == 0, 1.0, 2.0) / WIN
    backward = np.concatenate([np.cos(angle) * weight, np.sin(angle) * weight], axis=1) * taper
    return np.stack(two(forward)), np.stack(two(backward.T))


def chip_of(j):
    row, i = divmod(j, 4)
    z, q = divmod(row, 4)
    x = i if row % 2 == 0 else 3 - i
    y = q if z % 2 == 0 else 3 - q
    return x, y, z


def device_of(j, core):
    x, y, z = chip_of(j)
    return (((x // 2 * 4 + y) * 8 + z) * 2 + core) * 2 + x % 2


def permutes(windows):
    partner = [(device_of(j, c), device_of(j, 1 - c)) for j in range(windows) for c in (0, 1)]
    same, cross = [], []
    for j in range(windows - 1):
        same.append((device_of(j + 1, 0), device_of(j, 0)))
        same.append((device_of(j, 1), device_of(j + 1, 1)))
        cross.append((device_of(j + 1, 0), device_of(j, 1)))
        cross.append((device_of(j, 1), device_of(j + 1, 0)))
    return partner, same, cross


def flipped(pairs):
    return [(b, a) for a, b in pairs]


def core_index():
    return lax.rem(lax.axis_index("chan"), 2)


def split(value):
    hi = value.astype(BF16)
    return hi, (value - hi.astype(F32)).astype(BF16)


def stacked(value):
    hi, lo = split(value)
    return jnp.concatenate([hi, lo, hi], axis=0)


def dot(a, b):
    return jnp.dot(a, b, preferred_element_type=F32)


def plane_slot(b):
    j, core = divmod(b, 2)
    row, i = divmod(j, 4)
    x = i if row % 2 == 0 else 3 - i
    return x // 2, row, core, x % 2


def decimate_kernel(taps_hbm, raw_ref, out_ref, taps_ref, cur_ref, band_ref, stage_ref, in_sems, out_sems):
    planes = out_ref.shape[2]
    span = TAPS + DEC * BLK
    width = raw_ref.shape[1] // planes
    pair = 2
    loads = []
    for n in range(planes // pair):
        part = pl.ds(n * pair * width, pair * width)
        loads.append(pltpu.make_async_copy(raw_ref.at[:, part], cur_ref.at[:, part], in_sems.at[n]))
        loads[-1].start()
        if n == 0:
            taps_load = pltpu.make_async_copy(taps_hbm, taps_ref, in_sems.at[planes])
            taps_load.start()
    taps_load.wait()

    i = lax.broadcasted_iota(jnp.int32, (TAPS, TAPS), 0)
    j = lax.broadcasted_iota(jnp.int32, (TAPS, TAPS), 1)
    mirror = (i + j == TAPS - 1).astype(BF16)
    rows = jnp.broadcast_to(taps_ref[...].astype(F32), (BLK, TAPS))
    mirrored = dot(rows.astype(BF16), mirror)
    wide = jnp.concatenate([mirrored, jnp.zeros((BLK, span - TAPS), F32)], axis=1)
    wide = pltpu.roll(wide, 1, 1, stride=DEC, stride_axis=0)
    band_ref[...] = wide.T.astype(BF16)

    blocks = width // (DEC * BLK)
    group = 16
    band = band_ref[...]
    stores = []
    for plane in range(planes):
        if plane % pair == 0:
            loads[plane // pair].wait()
        for b0 in range(0, blocks, group):
            spans = []
            for b in range(b0, b0 + group):
                start = plane * width + b * DEC * BLK
                if start == 0:
                    tail = jnp.zeros((cur_ref.shape[0], TAPS), BF16)
                    spans.append(jnp.concatenate([tail, cur_ref[:, : DEC * BLK]], axis=1))
                else:
                    spans.append(cur_ref[:, start - TAPS : start + DEC * BLK])
            result = dot(jnp.concatenate(spans, axis=0), band)
            for n in range(group):
                xh, row, core, xl = plane_slot(b0 + n)
                y = row if plane % 2 == 0 else 3 - row
                stage_ref[plane, xh, y, core, xl] = result[n * 16 : (n + 1) * 16]
        stores.append(pltpu.make_async_copy(stage_ref.at[plane], out_ref.at[:, :, plane], out_sems.at[plane]))
        stores[-1].start()
    for store in stores:
        store.wait()


def decimate(raw, taps):
    channels, length = raw.shape
    planes = 8
    return pl.pallas_call(
        decimate_kernel,
        in_specs=[ANY, ANY],
        out_specs=ANY,
        out_shape=jax.ShapeDtypeStruct((2, 4, planes, 2, 2, channels, BLK), F32),
        scratch_shapes=[
            pltpu.VMEM((1, TAPS), BF16),
            pltpu.VMEM(raw.shape, BF16),
            pltpu.VMEM((TAPS + DEC * BLK, BLK), BF16),
            pltpu.VMEM((planes, 2, 4, 2, 2, channels, BLK), F32),
            pltpu.SemaphoreType.DMA((planes + 1,)),
            pltpu.SemaphoreType.DMA((planes,)),
        ],
        compiler_params=params(60),
        name="decimate",
    )(taps.reshape(1, TAPS), raw)


def unplane_kernel(in_ref, out_ref, stage_ref, sems):
    planes = in_ref.shape[2]
    pair = 2
    stores = []
    for plane in range(planes):
        for b in range(32):
            xh, row, core, xl = plane_slot(b)
            y = row if plane % 2 == 0 else 3 - row
            start = (plane * 32 + b) * BLK
            stage_ref[:, start : start + BLK] = in_ref[xh, y, plane, core, xl]
        if plane % pair == pair - 1:
            part = pl.ds((plane + 1 - pair) * 32 * BLK, pair * 32 * BLK)
            store = pltpu.make_async_copy(stage_ref.at[:, part], out_ref.at[:, part], sems.at[plane // pair])
            store.start()
            stores.append(store)
    for store in stores:
        store.wait()


def unplane(blocks):
    planes = blocks.shape[2]
    channels = blocks.shape[5]
    return pl.pallas_call(
        unplane_kernel,
        in_specs=[VMEM],
        out_specs=ANY,
        out_shape=jax.ShapeDtypeStruct((channels, planes * 32 * BLK), F32),
        scratch_shapes=[
            pltpu.VMEM((channels, planes * 32 * BLK), F32),
            pltpu.SemaphoreType.DMA((planes // 2,)),
        ],
        compiler_params=params(8),
        name="unplane",
    )(blocks)


def turn(value, k, n):
    re, im = value
    if 8 * abs(k) == n:
        c = np.float32(np.sqrt(0.5))
        return ((re - im) * c, (re + im) * c) if k > 0 else ((re + im) * c, (im - re) * c)
    c, s = np.float32(np.cos(2 * np.pi * k / n)), np.float32(np.sin(2 * np.pi * k / n))
    return re * c - im * s, re * s + im * c


def real_forward(load, n, start, step):
    if n == 2:
        a, b = load(start), load(start + step)
        return [a + b, a - b]
    even = real_forward(load, n // 2, start, 2 * step)
    odd = real_forward(load, n // 2, start + step, 2 * step)
    half, quarter = n // 2, n // 4
    out = [None] * (half + 1)
    out[0], out[half] = even[0] + odd[0], even[0] - odd[0]
    out[quarter] = (even[quarter], -odd[quarter])
    for k in range(1, quarter):
        re, im = turn(odd[k], -k, n)
        er, ei = even[k]
        out[k] = (er + re, ei + im)
        out[half - k] = (er - re, im - ei)
    return out


def real_inverse(bins):
    half = len(bins) - 1
    if half == 1:
        return [bins[0] + bins[1], bins[0] - bins[1]]
    n, quarter = 2 * half, half // 2
    even, odd = [bins[0] + bins[half]], [bins[0] - bins[half]]
    for k in range(1, quarter):
        (ar, ai), (br, bi) = bins[k], bins[half - k]
        even.append((ar + br, ai - bi))
        odd.append(turn((ar - br, ai + bi), k, n))
    re, im = bins[quarter]
    even.append(re + re)
    odd.append(-(im + im))
    out = [None] * n
    out[0::2], out[1::2] = real_inverse(even), real_inverse(odd)
    return out


def real_slot(core, chunk, i):
    s = chunk * WIDTH + i % WIDTH + (HALF if i >= WIDTH else 0)
    return lax.rem(s + HALF * core, SLOTS)


def second_stage(core, chunk, mid_ref, second_ref, own_ref, other_ref):
    for i in range(PART):
        s = real_slot(core, chunk, i)
        wave = dot(second_ref[s], stacked(mid_ref[s]))
        if i < WIDTH:
            own_ref[i] = wave
        else:
            other_ref[i - WIDTH] = wave


def forward_kernel(x_hbm, second_ref, own_ref, other_ref, mid_ref, x_ref, sems):
    half = ROOT // 2
    loads = []
    for n in range(2):
        part = pl.ds(n * half, half)
        loads.append(pltpu.make_async_copy(x_hbm.at[:, part], x_ref.at[:, part], sems.at[n]))
        loads[-1].start()

    def tile(t, carry):
        rows = pl.ds(pl.multiple_of(t * 8, 8), 8)
        rows_im = pl.ds(pl.multiple_of(ROOT + t * 8, 8), 8)
        bins = real_forward(lambda c1: x_ref[c1, rows, :], ROOT, 0, 1)
        mid_ref[0, rows, :] = bins[0]
        mid_ref[0, rows_im, :] = bins[SLOTS]
        for s in range(1, SLOTS):
            mid_ref[s, rows, :], mid_ref[s, rows_im, :] = bins[s]
        return carry

    for n in range(2):
        loads[n].wait()
        lax.fori_loop(n * half // 8, (n + 1) * half // 8, tile, 0, unroll=2)
    second_stage(core_index(), 0, mid_ref, second_ref, own_ref, other_ref)


def forward_space(x, second):
    return pl.pallas_call(
        forward_kernel,
        in_specs=[ANY, VMEM],
        out_specs=[VMEM] * 3,
        out_shape=[WAVE, WAVE, jax.ShapeDtypeStruct((SLOTS, BLK, BLK), F32)],
        scratch_shapes=[pltpu.VMEM((ROOT, ROOT, BLK), F32), pltpu.SemaphoreType.DMA((2,))],
        compiler_params=params(14),
        name="forward_space",
    )(x.reshape(ROOT, ROOT, BLK), second)


def forward_more_kernel(chunk, mid_ref, second_ref, own_ref, other_ref):
    second_stage(core_index(), chunk, mid_ref, second_ref, own_ref, other_ref)


def forward_more(chunk, middle, second):
    return pl.pallas_call(
        functools.partial(forward_more_kernel, chunk),
        in_specs=[VMEM] * 2,
        out_specs=[VMEM] * 2,
        out_shape=[WAVE, WAVE],
        compiler_params=params(12),
        name="forward_more",
    )(middle, second)


def inverse_stage(core, chunk, own_ref, halo_ref, part_ref, cross_ref, inv_ref, mid_ref):
    for i in range(PART):
        if i < WIDTH:
            z = own_ref[i] + halo_ref[i]
        else:
            z = part_ref[i - WIDTH] + cross_ref[i - WIDTH]
        mid_ref[i] = dot(inv_ref[real_slot(core, chunk, i)], stacked(z))


def inverse_more_kernel(chunk, own_ref, halo_ref, part_ref, cross_ref, inv_ref, mid_ref):
    inverse_stage(core_index(), chunk, own_ref, halo_ref, part_ref, cross_ref, inv_ref, mid_ref)


def inverse_more(chunk, waves, inv):
    return pl.pallas_call(
        functools.partial(inverse_more_kernel, chunk),
        in_specs=[VMEM] * 5,
        out_specs=VMEM,
        out_shape=MIDDLE,
        compiler_params=params(12),
        name="inverse_more",
    )(*waves, inv)


def inverse_kernel(own_ref, halo_ref, part_ref, cross_ref, inv_ref, *rest):
    earlier, out_ref, mid_ref = rest[:-2], rest[-2], rest[-1]
    core = core_index()
    inverse_stage(core, CHUNKS - 1, own_ref, halo_ref, part_ref, cross_ref, inv_ref, mid_ref)
    refs = earlier + (mid_ref,)

    def tile(t, carry):
        rows = pl.ds(pl.multiple_of(t * 8, 8), 8)
        rows_im = pl.ds(pl.multiple_of(ROOT + t * 8, 8), 8)

        def both(s):
            ref = refs[s % HALF // WIDTH]
            place = s % WIDTH + WIDTH * lax.rem(core + s // HALF, 2)
            return ref[place, rows, :], ref[place, rows_im, :]

        low, high = both(0)
        values = real_inverse([low] + [both(s) for s in range(1, SLOTS)] + [high])
        for c1 in range(ROOT):
            out_ref[c1, rows, :] = values[c1]
        return carry

    lax.fori_loop(0, ROOT // 8, tile, 0, unroll=2)


def inverse_space(waves, earlier, inv):
    return pl.pallas_call(
        inverse_kernel,
        in_specs=[VMEM] * (5 + len(earlier)),
        out_specs=VMEM,
        out_shape=jax.ShapeDtypeStruct((ROOT, ROOT, BLK), F32),
        scratch_shapes=[pltpu.VMEM(MIDDLE.shape, F32)],
        compiler_params=params(14),
        name="inverse_space",
    )(*waves, inv, *earlier)


def gains_kernel(gain_ref, band_ref, out_ref):
    core = core_index()
    n = ROOT // 2
    i = lax.broadcasted_iota(jnp.int32, (ROOT, ROOT), 0)
    j = lax.broadcasted_iota(jnp.int32, (ROOT, ROOT), 1)
    mirror = (i + j == ROOT - 1).astype(BF16)
    source = jnp.where(i == 0, 0, jnp.where(i < n, n - i, n + ROOT - 1 - i))
    mirror0 = (j == source).astype(BF16)

    def rows(k1, k2, count):
        return band_ref[pl.ds(k1 + ROOT * k2, count, stride=ROOT), :]

    def exact(perm, bands):
        return dot(perm, bands.astype(F32).astype(BF16))

    def pick(bands):
        total = jnp.zeros(bands.shape, F32)
        for b in range(BANDS):
            total = jnp.where(bands == b, gain_ref[b], total)
        return total

    def put(s, plus, minus):
        gp, gm = pick(plus.astype(F32)), pick(minus)
        out_ref[0, s] = gp + gm
        out_ref[1, s] = gp - gm

    for s in range(HALF):
        if s:
            k1 = s + HALF * core
            put(s, rows(k1, 0, ROOT), exact(mirror, rows(ROOT - k1, 0, ROOT)))
            continue

        @pl.when(core == 0)
        def _():
            plus = jnp.concatenate([rows(0, 0, n), rows(n, 0, n)], axis=0)
            minus = jnp.concatenate([rows(0, n, n), rows(n, n, n)], axis=0)
            put(0, plus, exact(mirror0, minus))

        @pl.when(core != 0)
        def _():
            put(0, rows(HALF, 0, ROOT), exact(mirror, rows(ROOT - HALF, 0, ROOT)))


def gains(band_gain, fan_band):
    return pl.pallas_call(
        gains_kernel,
        in_specs=[SMEM, VMEM],
        out_specs=VMEM,
        out_shape=jax.ShapeDtypeStruct((2, HALF, ROOT, BLK), F32),
        compiler_params=params(8),
        name="gains",
    )(band_gain, fan_band)


def time_kernel(first_chunk, *refs):
    own_ref, part_ref, same_ref, cross_ref, mine_ref, theirs_ref, fwd_ref, bwd_ref = refs[:8]
    out_refs = refs[8:]
    core, xl = core_index(), lax.axis_index("tile")
    step = pl.program_id(0)
    slots = own_ref.shape[0]
    rows = slots * BLK
    even = core == 0

    def flat(ref):
        return ref[...].reshape(rows, BLK)

    own, part, same, cross = flat(own_ref), flat(part_ref), flat(same_ref), flat(cross_ref)
    x = jnp.concatenate(
        [
            jnp.where(even, cross, same),
            jnp.where(even, own, part),
            jnp.where(even, part, own),
            jnp.where(even, same, cross),
        ],
        axis=1,
    )
    hi, lo = split(x)
    fwd_hi = fwd_ref[0]
    v = dot(hi, fwd_hi) + dot(lo, fwd_hi) + dot(hi, fwd_ref[1])
    pieces = []
    for s in range(slots):
        p = v[s * BLK : s * BLK + ROOT]
        q = v[s * BLK + ROOT : (s + 1) * BLK]
        a, d = p[:, :BINS], p[:, BINS:]
        c, b = q[:, :BINS], q[:, BINS:]

        def wide(kind):
            mine, theirs = mine_ref[kind, s], theirs_ref[kind, s]
            low = jnp.where(xl == 0, mine, theirs)
            high = jnp.where(xl == 0, theirs, mine)
            return jnp.concatenate([low, high], axis=1)

        gs, gd = wide(0), wide(1)
        gr = gi = gs
        if s == 0 and first_chunk:
            row = lax.broadcasted_iota(jnp.int32, (ROOT, BINS), 0)
            pair = (row == 0) & (step == 0) & even
            gr = jnp.where(pair, gs + gd, gs)
            gi = jnp.where(pair, gs - gd, gs)
            gd = jnp.where(pair, 0.0, gd)
        pieces.append(jnp.concatenate([gr * a + gd * b, gr * d - gd * c], axis=1))
        pieces.append(jnp.concatenate([gi * c - gd * d, gd * a + gi * b], axis=1))
    hi, lo = split(jnp.concatenate(pieces, axis=0))
    bwd_hi = bwd_ref[0]
    z = dot(hi, bwd_hi) + dot(lo, bwd_hi) + dot(hi, bwd_ref[1])
    before, low, high, after = (z[:, n * BLK : (n + 1) * BLK] for n in range(4))
    outs = [
        jnp.where(even, low, high),
        jnp.where(even, high, low),
        jnp.where(even, after, before),
        jnp.where(even, before, after),
    ]
    for out_ref, value in zip(out_refs, outs):
        out_ref[...] = value.reshape(slots, BLK, BLK)


def time_filter(chunk, waves, mine, theirs, fwd, bwd):
    slots = 8
    steps = WIDTH // slots
    data = pl.BlockSpec((slots, BLK, BLK), lambda g: (g, 0, 0))
    gain = pl.BlockSpec((2, slots, ROOT, BLK), lambda g: (0, chunk * steps + g, 0, 0))
    table = pl.BlockSpec((2, WIN, WIN), lambda g: (0, 0, 0))
    return pl.pallas_call(
        functools.partial(time_kernel, chunk == 0),
        grid=(steps,),
        in_specs=[data] * 4 + [gain] * 2 + [table] * 2,
        out_specs=[data] * 4,
        out_shape=[jax.ShapeDtypeStruct((WIDTH, BLK, BLK), F32)] * 4,
        compiler_params=params(24),
        name="time_filter",
    )(*waves, mine, theirs, fwd, bwd)


def body(raw_strain, fir_taps, fan_band, band_gain):
    second, inverse = (jnp.asarray(t) for t in spatial_tables())
    fwd, bwd = (jnp.asarray(t) for t in temporal_tables())
    partner, same, cross = permutes(raw_strain.shape[1] // DEC // HOP)

    mine = gains(band_gain, fan_band)
    theirs = lax.ppermute(mine, "tile", [(0, 1), (1, 0)])

    blocks = decimate(raw_strain, fir_taps)
    shape = blocks.shape
    blocks = blocks.reshape((256,) + shape[5:])
    blocks = lax.all_to_all(blocks, AXES, 0, 0, tiled=True)
    own, other, middle = forward_space(blocks, second)
    received = []
    for g in range(CHUNKS):
        if g:
            own, other = forward_more(g, middle, second)
        from_partner = lax.ppermute(other, AXES, partner)
        from_same = lax.ppermute(own, AXES, same)
        from_cross = lax.ppermute(other, AXES, cross)
        received.append((own, from_partner, from_same, from_cross))
    returned = []
    for g in range(CHUNKS):
        own, part, halo, far = time_filter(g, received[g], mine, theirs, fwd, bwd)
        back_partner = lax.ppermute(part, AXES, partner)
        back_same = lax.ppermute(halo, AXES, flipped(same))
        back_cross = lax.ppermute(far, AXES, flipped(cross))
        returned.append((own, back_same, back_partner, back_cross))
    earlier = [inverse_more(g, returned[g], inverse) for g in range(CHUNKS - 1)]
    filtered = inverse_space(returned[-1], earlier, inverse)
    filtered = lax.all_to_all(filtered.reshape(256, 16, BLK), AXES, 0, 0, tiled=True)
    return unplane(filtered.reshape(shape))


def solution(mesh):
    return jax.shard_map(
        body,
        mesh=mesh,
        in_specs=(P(AXES, None), P(), P(None, "tile"), P()),
        out_specs=P(AXES, None),
        check_vma=False,
    )
```
